128 devices in a mesh: blk: 16 (over x_hi, z, core), narrow: 8 (over y, x_lo).
Axes of the slice: x: 4 (x_hi: 2, x_lo: 2; x = x_hi * 2 + x_lo), y: 4, z: 4, core: 2. Of those that a mesh axis runs over, the one named last changes fastest.
Arguments:
- points: float32 [32, 65536], P(None, ('blk', 'narrow')), may hold values from -4.5 to 4.5
- lengthscale: float32 [32], replicated, may hold values from 2.5 to 5
- noise: float32 [1], replicated, may hold values from 0.3 to 1
- solution: float32 [17, 65536], P(None, ('blk', 'narrow')), may hold values from -6 to 6
- residual: float32 [17, 65536], P(None, ('blk', 'narrow')), may hold values from -6 to 6
- direction: float32 [17, 65536], P(None, ('blk', 'narrow')), may hold values from -6 to 6
Outputs:
- new_solution: float32 [17, 65536], P(None, ('blk', 'narrow'))
- new_residual: float32 [17, 65536], P(None, ('blk', 'narrow'))
- new_direction: float32 [17, 65536], P(None, ('blk', 'narrow'))
The draws below stay inside these ranges and needn't reach their ends.
All inputs are finite; a program needn't handle non-finite values.
Results may differ from the reference program's by a relative error of at most 0.000086.
Values sent between devices are 32-bit elements; how exact they have to be, the bound alone decides.
A program may use at most 64 MiB of HBM per device.

```python
import math
import jax
import jax.numpy as jnp
from jax import lax

DIM = 32
RHS = 17
POINTS = 65536


def draw_points(key, part):
    key = jax.random.fold_in(key, 11)
    centre_key, label_key, spread_key = jax.random.split(key, 3)
    centre_count = 128
    labels = jax.random.randint(label_key, (POINTS,), 0, centre_count)
    centres = jnp.clip(jax.random.normal(centre_key, (DIM, centre_count), jnp.float32), -3.0, 3.0)
    spread = 0.35 * jnp.clip(jax.random.normal(spread_key, (DIM, POINTS), jnp.float32), -3.0, 3.0)
    return (jnp.take(centres, labels, axis=1) + spread).astype(jnp.float32)


def steps_of(stream_key, dims, shards, smallest, top_value):
    factor_of, own = 1.0, jax.random.fold_in(stream_key, 6)
    for position, blocks in shards:
        draws = jnp.exp(jax.random.uniform(jax.random.fold_in(own, position), (blocks,), jnp.float32, smallest / len(shards), top_value / len(shards)))
        factor_of = factor_of * jnp.repeat(draws, dims[position] // blocks).reshape([-1 if axis == position else 1 for axis in range(len(dims))])
    return factor_of


def centred(own_key, dims, scale, most, shards=(), dtype=jnp.bfloat16):
    gain = steps_of(own_key, dims, shards, -0.22, 0.18) if shards else 1.0
    values = jax.random.normal(own_key, dims, jnp.float32) * scale * gain
    return jnp.minimum(jnp.maximum(values, -most), most).astype(dtype)


def setup_inputs(seed: int = 0) -> dict:
    key_list = jax.random.split(jax.random.key(seed), 7)
    return {
        "points": draw_points(jax.random.fold_in(key_list[6], 71), 0),
        "lengthscale": jnp.clip(jnp.exp(jax.random.uniform(key_list[1], (DIM,), jnp.float32, math.log(2.5), math.log(5.0))), 2.5, 5.0),
        "noise": jnp.clip(jax.random.uniform(key_list[2], (1,), jnp.float32, 0.3, 1.0), 0.3, 1.0),
        "solution": centred(key_list[3], (RHS, POINTS), 1.0, 6.0, ((1, 128),), jnp.float32),
        "residual": centred(key_list[4], (RHS, POINTS), 1.0, 6.0, ((1, 128),), jnp.float32),
        "direction": centred(key_list[5], (RHS, POINTS), 1.0, 6.0, ((1, 128),), jnp.float32),
    }


def matern(cross, sq_rows, sq_cols):
    squared = jnp.maximum(sq_rows[:, None] + sq_cols[None, :] - 2.0 * cross, 0.0)
    scaled_dist = jnp.sqrt(squared) * math.sqrt(5.0)
    return (1.0 + scaled_dist + scaled_dist * scaled_dist / 3.0) * jnp.exp(-scaled_dist)

def gram(left, right):
    return lax.dot_general(left, right, (((1,), (1,)), ((), ())), precision=lax.Precision.HIGHEST)

def reference(points, lengthscale, noise, solution, residual, direction):
    scaled = points / lengthscale[:, None]
    squares = lax.optimization_barrier(jnp.sum(scaled * scaled, 0))
    piece = math.gcd(POINTS, 1024)
    count = POINTS // piece
    row_sets = scaled.reshape(DIM, count, piece).transpose(1, 0, 2)
    sq_sets = squares.reshape(count, piece)

    def one_set(item):
        cross = lax.dot_general(item[0], scaled, (((0,), (0,)), ((), ())), precision=lax.Precision.HIGHEST)
        kern = matern(cross, item[1], squares)
        return gram(direction, kern)
    parts = lax.map(one_set, (row_sets, sq_sets))
    image = parts.transpose(1, 0, 2).reshape(RHS, POINTS) + noise[0] * direction
    curvature = gram(direction, image)
    correlation = gram(direction, residual)
    factor = jnp.linalg.cholesky(curvature)
    step_coef = jax.scipy.linalg.cho_solve((factor, True), correlation)
    hi = lax.Precision.HIGHEST
    new_solution = solution + jnp.dot(step_coef.T, direction, precision=hi)
    new_residual = residual - jnp.dot(step_coef.T, image, precision=hi)
    update = gram(image, new_residual)
    conj_coef = -jax.scipy.linalg.cho_solve((factor, True), update)
    new_direction = new_residual + jnp.dot(conj_coef.T, direction, precision=hi)
    return (new_solution, new_residual, new_direction)
```

```python
import functools
import math

import jax
import jax.numpy as jnp
from jax import lax
from jax.experimental import pallas as pl
from jax.experimental.pallas import tpu as pltpu
from jax.sharding import PartitionSpec as P

BF16 = jnp.bfloat16
F32 = jnp.float32
LN2 = math.log(2.0)
MESH = pl.DeviceIdType.MESH
FEATS = 32
SIDES = 17
SIDES_PAD = 24
PTS = 512
BLK = 16
NARROW = 8
HALF = BLK // 2
PACKET = 56
DEPTH = 256
CHUNK = 2048


def dot(left, right, dims=((1,), (0,))):
    return lax.dot_general(left, right, (dims, ((), ())), preferred_element_type=F32)


def exact_dot(left, right, dims=((1,), (0,))):
    return lax.dot_general(
        left, right, (dims, ((), ())), precision=lax.Precision.HIGHEST, preferred_element_type=F32
    )


def split3(x):
    first = x.astype(BF16).astype(F32)
    second = (x - first).astype(BF16).astype(F32)
    third = (x - first - second).astype(BF16).astype(F32)
    return first, second, third


def norm_rows(squares, norms_first):
    s1, s2, s3 = split3(squares)
    row = lax.broadcasted_iota(jnp.int32, (16, PTS), 0)
    zero = jnp.zeros((16, PTS), F32)
    base = 0 if norms_first else 3
    ones = 3 if norms_first else 0
    out = jnp.where((row >= ones) & (row < ones + 3), 1.0, zero)
    for place, part in enumerate((s1, s2, s3)):
        out = jnp.where(row == base + place, jnp.broadcast_to(part, (16, PTS)), out)
    return out


def expand(pts, left):
    p1, p2, p3 = split3(pts)
    squares = jnp.sum(pts * pts, 0, keepdims=True)
    order = (p1, p1, p2, p2, p1, p3) if left else (p1, p2, p1, p2, p3, p1)
    scale = -2.0 if left else 1.0
    rows = [part * scale for part in order]
    rows.append(norm_rows(squares, left))
    rows.append(jnp.zeros((DEPTH - 6 * FEATS - 16, PTS), F32))
    return jnp.concatenate(rows, 0)


def split_dir(rows):
    hi = rows.astype(BF16).astype(F32)
    return jnp.concatenate([hi, rows - hi], 0).astype(BF16)


def matern(q):
    q = jnp.maximum(q, 1e-30)
    t = q * lax.rsqrt(q)
    s = t + 1.5 / LN2
    return (s * s + 0.75 / LN2**2) * jnp.exp2(-t)


def kernel(points, scale, noise, solution, residual, direction, new_solution, new_residual, new_direction,
           pkt, gat, cols, left, ldir, right, rdir, fwd, back, rsend, rrecv, bsend, brecv, dir24, res24, img24,
           gram, ar1, ar2, own,
           gat_send, gat_recv, col_send, col_recv, r_send, r_recv, b_send, b_recv,
           ar1_send, ar1_recv, ar2_send, ar2_recv):
    b = lax.axis_index("blk")
    n = lax.axis_index("narrow")

    def narrow_peer(offset):
        return (b, lax.rem(n + offset, NARROW))

    def blk_peer(offset):
        return (lax.rem(b + offset, BLK), n)

    barrier = pltpu.get_barrier_semaphore()
    for j in range(1, NARROW):
        pl.semaphore_signal(barrier, inc=1, device_id=narrow_peer(j), device_id_type=MESH)
    for k in range(1, BLK):
        pl.semaphore_signal(barrier, inc=1, device_id=blk_peer(k), device_id_type=MESH)

    dir24[...] = jnp.zeros_like(dir24)
    dir24[0:SIDES, :] = direction[...]
    res24[...] = jnp.zeros_like(res24)
    res24[0:SIDES, :] = residual[...]
    pkt[0:FEATS, :] = points[...] * scale[...]
    pkt[FEATS:PACKET, :] = dir24[...]
    pl.semaphore_wait(barrier, NARROW + BLK - 2)

    def gather_copy(j):
        return pltpu.make_async_remote_copy(
            src_ref=pkt, dst_ref=gat.at[j], send_sem=gat_send.at[j], recv_sem=gat_recv.at[j],
            device_id=narrow_peer(NARROW - j), device_id_type=MESH)

    def column_copy(k):
        return pltpu.make_async_remote_copy(
            src_ref=pkt, dst_ref=cols.at[k], send_sem=col_send.at[k], recv_sem=col_recv.at[k],
            device_id=blk_peer(BLK - k), device_id_type=MESH)

    def forward_copy(k):
        return pltpu.make_async_remote_copy(
            src_ref=rsend.at[k], dst_ref=rrecv.at[k], send_sem=r_send.at[k], recv_sem=r_recv.at[k],
            device_id=blk_peer(k), device_id_type=MESH)

    def back_copy(j):
        return pltpu.make_async_remote_copy(
            src_ref=bsend.at[j], dst_ref=brecv.at[j], send_sem=b_send.at[j], recv_sem=b_recv.at[j],
            device_id=narrow_peer(j), device_id_type=MESH)

    for j in range(1, NARROW):
        gather_copy(j).start()
    for k in range(1, HALF + 1):
        column_copy(k).start()

    def load_right(packet):
        right[...] = expand(packet[0:FEATS, :], False).astype(BF16)
        rdir[...] = split_dir(packet[FEATS:PACKET, :])

    def load_left(j, packet):
        at = pl.ds(pl.multiple_of(j * PTS, PTS), PTS)
        left[at, :] = expand(packet[0:FEATS, :], True).T.astype(BF16)
        ldir[:, at] = split_dir(packet[FEATS:PACKET, :])

    def tile(start, size):
        at = pl.ds(pl.multiple_of(start, PTS), size)
        kern = matern(dot(left[at, :], right[...]))
        hi = kern.astype(BF16)
        lo = (kern - hi.astype(F32)).astype(BF16)
        sides = ldir[:, at]
        fwd[...] += dot(sides, hi) + dot(sides, lo)
        back[at, :] += dot(hi, rdir[...], ((1,), (1,))) + dot(lo, rdir[...], ((1,), (1,)))

    back[...] = jnp.zeros_like(back)
    fwd[...] = jnp.zeros_like(fwd)
    load_right(pkt)
    load_left(0, pkt)
    tile(0, PTS)

    @pl.loop(1, NARROW)
    def _(j):
        gather_copy(j).wait_recv()
        load_left(j, gat.at[j])

        @pl.when(j <= NARROW // 2)
        def _():
            tile(j * PTS, PTS)

    own[...] = fwd[0:SIDES_PAD, :] + fwd[SIDES_PAD:, :]
    back[0:PTS, :] = jnp.zeros((PTS, 2 * SIDES_PAD), F32)
    back[NARROW // 2 * PTS:(NARROW // 2 + 1) * PTS, :] = jnp.zeros((PTS, 2 * SIDES_PAD), F32)

    upper = jnp.where(b >= HALF, PTS, 0)

    @pl.loop(1, HALF + 1)
    def _(k):
        column_copy(k).wait_recv()
        load_right(cols.at[k])
        fwd[...] = jnp.zeros_like(fwd)
        tile(jnp.where(k == HALF, upper, 0), CHUNK)

        @pl.when(k < HALF)
        def _():
            tile(CHUNK, CHUNK)

        rsend[k] = fwd[0:SIDES_PAD, :] + fwd[SIDES_PAD:, :]
        forward_copy(k).start()

    def back_slice(j):
        part = back[pl.ds(pl.multiple_of(j * PTS, PTS), PTS), :].T
        return part[0:SIDES_PAD, :] + part[SIDES_PAD:, :]

    @pl.loop(1, NARROW)
    def _(j):
        bsend[j] = back_slice(j)
        back_copy(j).start()

    own[...] += back_slice(0)
    for k in range(1, HALF + 1):
        forward_copy(k).wait_recv()
        own[...] += rrecv[k]
    for j in range(1, NARROW):
        back_copy(j).wait_recv()
        own[...] += brecv[j]
    img24[...] = own[...] * (LN2 * LN2 / 3.0) + noise[...] * dir24[...]

    zeros8 = jnp.zeros((8, PTS), F32)
    zeros64 = jnp.zeros((64, PTS), F32)
    img, dirs, res = img24[...], dir24[...], res24[...]
    table = jnp.concatenate([dirs, zeros8, img, zeros8, zeros64], 0)
    other = jnp.concatenate([zeros64, img, zeros8, dirs, zeros8], 0)
    gram[...] = exact_dot(img, table, ((1,), (1,))) + exact_dot(res, other, ((1,), (1,)))

    def ar1_copy(j):
        return pltpu.make_async_remote_copy(
            src_ref=gram, dst_ref=ar1.at[n], send_sem=ar1_send.at[j], recv_sem=ar1_recv.at[j],
            device_id=narrow_peer(j), device_id_type=MESH)

    for j in range(1, NARROW):
        ar1_copy(j).start()
    ar1[n] = gram[...]
    for j in range(1, NARROW):
        ar1_copy(j).wait()
    total = ar1[0]
    for j in range(1, NARROW):
        total = total + ar1[j]
    gram[...] = total

    def ar2_copy(k):
        return pltpu.make_async_remote_copy(
            src_ref=gram, dst_ref=ar2.at[b], send_sem=ar2_send.at[k], recv_sem=ar2_recv.at[k],
            device_id=blk_peer(k), device_id_type=MESH)

    for k in range(1, BLK):
        ar2_copy(k).start()
    ar2[b] = gram[...]
    for k in range(1, BLK):
        ar2_copy(k).wait()
    total = ar2[0]
    for k in range(1, BLK):
        total = total + ar2[k]

    curv = total[:, 0:SIDES_PAD]
    curv = 0.5 * (curv + curv.T)
    outer = pltpu.roll(total, 96, 1)[:, 0:SIDES_PAD]
    img_res = pltpu.roll(total, 64, 1)[:, 0:SIDES_PAD]
    dir_res = pltpu.roll(total, 32, 1)[:, 0:SIDES_PAD]
    row = lax.broadcasted_iota(jnp.int32, (SIDES_PAD, SIDES_PAD), 0)
    col = lax.broadcasted_iota(jnp.int32, (SIDES_PAD, SIDES_PAD), 1)
    inverse = (row == col).astype(F32)
    for i in range(SIDES):
        pivot = 1.0 / curv[i:i + 1, i:i + 1]
        head = curv[i:i + 1, :] * pivot
        tail = inverse[i:i + 1, :] * pivot
        factor = jnp.where(row[:, 0:1] == i, 0.0, curv[:, i:i + 1])
        curv = jnp.where(row == i, head, curv - factor * head)
        inverse = jnp.where(row == i, tail, inverse - factor * tail)

    step_t = exact_dot(dir_res, inverse)
    conj_t = exact_dot(exact_dot(step_t, outer) - img_res, inverse)
    res_new = res - exact_dot(step_t, img)
    new_solution[...] = solution[...] + exact_dot(step_t, dirs)[0:SIDES, :]
    new_residual[...] = res_new[0:SIDES, :]
    new_direction[...] = (res_new + exact_dot(conj_t, dirs))[0:SIDES, :]

    for j in range(1, NARROW):
        gather_copy(j).wait_send()
        back_copy(j).wait_send()
    for k in range(1, HALF + 1):
        column_copy(k).wait_send()
        forward_copy(k).wait_send()


def on_device(points, lengthscale, noise, solution, residual, direction):
    scale = (math.sqrt(5.0) / LN2 / lengthscale)[:, None]
    vmem = pl.BlockSpec(memory_space=pltpu.VMEM)
    sem = pltpu.SemaphoreType.DMA
    rows = NARROW * PTS
    return pl.pallas_call(
        kernel,
        out_shape=[jax.ShapeDtypeStruct((SIDES, PTS), F32)] * 3,
        in_specs=[vmem] * 6,
        out_specs=[vmem] * 3,
        scratch_shapes=[
            pltpu.VMEM((PACKET, PTS), F32),
            pltpu.VMEM((NARROW, PACKET, PTS), F32),
            pltpu.VMEM((HALF + 1, PACKET, PTS), F32),
            pltpu.VMEM((rows, DEPTH), BF16),
            pltpu.VMEM((2 * SIDES_PAD, rows), BF16),
            pltpu.VMEM((DEPTH, PTS), BF16),
            pltpu.VMEM((2 * SIDES_PAD, PTS), BF16),
            pltpu.VMEM((2 * SIDES_PAD, PTS), F32),
            pltpu.VMEM((rows, 2 * SIDES_PAD), F32),
            pltpu.VMEM((HALF + 1, SIDES_PAD, PTS), F32),
            pltpu.VMEM((HALF + 1, SIDES_PAD, PTS), F32),
            pltpu.VMEM((NARROW, SIDES_PAD, PTS), F32),
            pltpu.VMEM((NARROW, SIDES_PAD, PTS), F32),
            pltpu.VMEM((SIDES_PAD, PTS), F32),
            pltpu.VMEM((SIDES_PAD, PTS), F32),
            pltpu.VMEM((SIDES_PAD, PTS), F32),
            pltpu.VMEM((SIDES_PAD, 128), F32),
            pltpu.VMEM((NARROW, SIDES_PAD, 128), F32),
            pltpu.VMEM((BLK, SIDES_PAD, 128), F32),
            pltpu.VMEM((SIDES_PAD, PTS), F32),
            sem((NARROW,)), sem((NARROW,)), sem((HALF + 1,)), sem((HALF + 1,)),
            sem((HALF + 1,)), sem((HALF + 1,)), sem((NARROW,)), sem((NARROW,)),
            sem((NARROW,)), sem((NARROW,)), sem((BLK,)), sem((BLK,)),
        ],
        compiler_params=pltpu.CompilerParams(
            collective_id=0, has_side_effects=True, vmem_limit_bytes=56 * 2**20
        ),
        cost_estimate=pl.CostEstimate(flops=30_000_000_000, bytes_accessed=1_000_000, transcendentals=34_000_000),
        name="block_cg",
    )(points, scale, noise.reshape(1, 1), solution, residual, direction)


def solution(mesh):
    placed = P(None, ("blk", "narrow"))
    return jax.shard_map(
        on_device,
        mesh=mesh,
        in_specs=(placed, P(), P(), placed, placed, placed),
        out_specs=(placed, placed, placed),
        check_vma=False,
    )
```

```python
import functools
import math

import jax
import jax.numpy as jnp
from jax import lax
from jax.experimental import pallas as pl
from jax.experimental.pallas import tpu as pltpu
from jax.sharding import PartitionSpec as P

BF16 = jnp.bfloat16
F32 = jnp.float32
LN2 = math.log(2.0)
MESH = pl.DeviceIdType.MESH
FEATS = 32
SIDES = 17
SIDES_PAD = 24
PTS = 512
ROWS = 8
PLANE = 16
SIDE = 4
FULL = 6
OFFSETS = ((1, 0), (0, 3), (1, 1), (3, 1), (2, 3), (3, 2), (2, 0), (0, 2), (2, 2))
COLS = len(OFFSETS)
STEP_X = tuple(dx for dx, _ in OFFSETS)
STEP_Z = tuple(dz for _, dz in OFFSETS)
PACKET = 56
DEPTH = 256
CHUNK = 2048
LANES = 128
LOW = 32
BOOST = 14
F8 = jnp.float8_e4m3fn
F8_TOP = 256.0


def dot(left, right, dims=((1,), (0,))):
    return lax.dot_general(left, right, (dims, ((), ())), preferred_element_type=F32)


def exact_dot(left, right, dims=((1,), (0,))):
    return lax.dot_general(
        left, right, (dims, ((), ())), precision=lax.Precision.HIGHEST, preferred_element_type=F32
    )


def split3(x):
    first = x.astype(BF16).astype(F32)
    second = (x - first).astype(BF16).astype(F32)
    third = (x - first - second).astype(BF16).astype(F32)
    return first, second, third


def norm_rows(squares, norms_first):
    s1, s2, s3 = split3(squares)
    row = lax.broadcasted_iota(jnp.int32, (16, PTS), 0)
    zero = jnp.zeros((16, PTS), F32)
    base = 0 if norms_first else 3
    ones = 3 if norms_first else 0
    out = jnp.where((row >= ones) & (row < ones + 3), 1.0, zero)
    for place, part in enumerate((s1, s2, s3)):
        out = jnp.where(row == base + place, jnp.broadcast_to(part, (16, PTS)), out)
    return out


def expand(pts, left):
    p1, p2, p3 = split3(pts)
    squares = jnp.sum(pts * pts, 0, keepdims=True)
    order = (p1, p1, p2, p2, p1, p3) if left else (p1, p2, p1, p2, p3, p1)
    scale = -2.0 if left else 1.0
    rows = [part * scale for part in order]
    rows.append(norm_rows(squares, left))
    rows.append(jnp.zeros((DEPTH - 6 * FEATS - 16, PTS), F32))
    return jnp.concatenate(rows, 0)


def split_dir(rows):
    hi = rows.astype(BF16).astype(F32)
    return jnp.concatenate([hi, rows - hi], 0).astype(BF16)


def matern(q):
    q = jnp.maximum(q, 1e-30)
    t = q * lax.rsqrt(q)
    return ((q + 3.0 / LN2**2) + t * (3.0 / LN2)) * jnp.exp2(BOOST - t)


def pick(k, values):
    if isinstance(k, int):
        return values[k - 1]
    out = values[0]
    for place, value in enumerate(values[1:], 2):
        out = jnp.where(k == place, value, out)
    return out


def kernel(points, scale, noise, solution, residual, direction, new_solution, new_residual, new_direction,
           pkt, gat, cols, left, ldir, ldirf, ldir8, lscale, right, rdir, rdir8, rscale, fwds, back, rsend, rrecv, bsend, brecv, dir24, res24, img24,
           gram, ar1, ar2, own,
           gat_send, gat_recv, col_send, col_recv, r_send, r_recv, b_send, b_recv,
           ar1_send, ar1_recv, ar2_send, ar2_recv):
    b = lax.axis_index("blk")
    n = lax.axis_index("narrow")

    x = b // 8 * 2 + n % 2
    z = b // 2 % SIDE
    m = n // 2 * 2 + b % 2

    def device(x, z, m):
        return (x // 2 * 8 + z * 2 + m % 2, m // 2 * 2 + x % 2)

    def row_peer(j):
        return device(x, z, lax.rem(m + j, ROWS))

    def plane_peer(dx, dz):
        return device(lax.rem(x + dx, SIDE), lax.rem(z + dz, SIDE), m)

    others = [(dx, dz) for dx in range(SIDE) for dz in range(SIDE) if dx or dz]

    barrier = pltpu.get_barrier_semaphore()
    for j in range(1, ROWS):
        pl.semaphore_signal(barrier, inc=1, device_id=row_peer(j), device_id_type=MESH)
    for dx, dz in others:
        pl.semaphore_signal(barrier, inc=1, device_id=plane_peer(dx, dz), device_id_type=MESH)

    dir24[...] = jnp.zeros_like(dir24)
    dir24[0:SIDES, :] = direction[...]
    res24[...] = jnp.zeros_like(res24)
    res24[0:SIDES, :] = residual[...]
    pkt[0:FEATS, :] = points[...] * scale[...]
    pkt[FEATS:PACKET, :] = dir24[...]
    pl.semaphore_wait(barrier, ROWS + PLANE - 2)

    def gather_copy(j):
        return pltpu.make_async_remote_copy(
            src_ref=pkt, dst_ref=gat.at[j], send_sem=gat_send.at[j], recv_sem=gat_recv.at[j],
            device_id=row_peer(ROWS - j), device_id_type=MESH)

    def column_copy(k):
        return pltpu.make_async_remote_copy(
            src_ref=pkt, dst_ref=cols.at[k], send_sem=col_send.at[k], recv_sem=col_recv.at[k],
            device_id=plane_peer(SIDE - pick(k, STEP_X), SIDE - pick(k, STEP_Z)), device_id_type=MESH)

    def forward_copy(k):
        return pltpu.make_async_remote_copy(
            src_ref=rsend.at[k], dst_ref=rrecv.at[k], send_sem=r_send.at[k], recv_sem=r_recv.at[k],
            device_id=plane_peer(pick(k, STEP_X), pick(k, STEP_Z)), device_id_type=MESH)

    def back_copy(j):
        return pltpu.make_async_remote_copy(
            src_ref=bsend.at[j], dst_ref=brecv.at[j], send_sem=b_send.at[j], recv_sem=b_recv.at[j],
            device_id=row_peer(j), device_id_type=MESH)

    middle = ROWS // 2
    for j in range(1, middle + 1):
        gather_copy(j).start()
    for k in range(1, COLS + 1):
        column_copy(k).start()

    def load_right(packet):
        right[...] = expand(packet[0:FEATS, :], False).astype(BF16)
        rows = packet[FEATS:PACKET, :]
        hi = rows.astype(BF16).astype(F32)
        spare = jnp.zeros((LANES - 2 * SIDES_PAD, PTS), F32)
        rdir[...] = jnp.concatenate([hi, rows - hi, spare], 0).T.astype(BF16)
        plain = jnp.concatenate([rows, jnp.zeros((LANES - SIDES_PAD, PTS), F32)], 0).T
        top = jnp.maximum(jnp.max(jnp.abs(plain), 0, keepdims=True), 1e-30)
        rdir8[...] = (plain * (F8_TOP / top)).astype(F8)
        rscale[...] = jnp.broadcast_to(top * (1.0 / F8_TOP), (8, LANES))

    def scale_left(at):
        rows = ldirf[:, at]
        top = jnp.maximum(jnp.max(jnp.abs(rows), 1, keepdims=True), 1e-30)
        ldir8[:, at] = (rows * (F8_TOP / top)).astype(F8)
        lscale[...] = jnp.broadcast_to(top * (1.0 / F8_TOP), (LOW, LANES))

    def load_left(j, packet):
        at = pl.ds(pl.multiple_of(j * PTS, PTS), PTS)
        left[at, :] = expand(packet[0:FEATS, :], True).T.astype(BF16)
        rows = packet[FEATS:PACKET, :]
        ldir[:, at] = split_dir(rows)
        ldirf[:, at] = jnp.concatenate([rows, jnp.zeros((LOW - SIDES_PAD, PTS), F32)], 0)
        return at

    def tile(k, start, size):
        at = pl.ds(pl.multiple_of(start, PTS), size)
        kern = matern(dot(left[at, :], right[...]))
        hi = kern.astype(BF16)
        lo = (kern - hi.astype(F32)).astype(F8)
        back[at, :] += dot(hi, rdir[...])
        back[at, :] += dot(lo, rdir8[...]) * rscale[0:1, :]
        fwds[k] += dot(ldir[:, at], hi)
        fwds[k, 0:LOW] += dot(ldir8[:, at], lo) * lscale[:, 0:1]

    back[...] = jnp.zeros_like(back)
    fwds[...] = jnp.zeros_like(fwds)
    load_right(pkt)

    @pl.loop(0, middle + 1)
    def _(j):
        @pl.when(j > 0)
        def _():
            gather_copy(j).wait_recv()

        @pl.when(j == 0)
        def _():
            gat[0] = pkt[...]

        scale_left(load_left(j, gat.at[j]))
        tile(0, j * PTS, PTS)

    own[...] = fwds[0, 0:SIDES_PAD] + fwds[0, SIDES_PAD:]
    back[0:PTS, :] = jnp.zeros((PTS, LANES), F32)
    back[middle * PTS:(middle + 1) * PTS, :] = jnp.zeros((PTS, LANES), F32)
    scale_left(pl.ds(0, (middle + 1) * PTS))
    upper_x = jnp.where(x >= SIDE // 2, PTS, 0)
    upper_z = jnp.where(z >= SIDE // 2, PTS, 0)

    def back_slice(j):
        part = back[pl.ds(pl.multiple_of(j * PTS, PTS), PTS), :].T
        return part[0:SIDES_PAD, :] + part[SIDES_PAD:2 * SIDES_PAD, :]

    def send_back(first, last):
        @pl.loop(first, last)
        def _(j):
            bsend[j] = back_slice(j)
            back_copy(j).start()

    @pl.loop(0, COLS + FULL)
    def _(s):
        first = s < COLS
        k = jnp.where(first, s + 1, COLS + FULL - s)

        @pl.when(first)
        def _():
            column_copy(k).wait_recv()

        @pl.when((s >= 1) & (s < ROWS - middle))
        def _():
            gather_copy(s + middle).start()

        @pl.when(s == COLS)
        def _():
            @pl.loop(middle + 1, ROWS)
            def _(j):
                gather_copy(j).wait_recv()
                load_left(j, gat.at[j])

            scale_left(pl.ds(middle * PTS, (ROWS - middle) * PTS))
            send_back(1, middle)

        load_right(cols.at[k])
        upper = jnp.where(k == FULL + 2, upper_z, upper_x)
        tile(k, jnp.where(first, jnp.where(k > FULL, upper, 0), CHUNK), CHUNK)

        @pl.when(s >= FULL)
        def _():
            rsend[k] = fwds[k, 0:SIDES_PAD] + fwds[k, SIDES_PAD:]
            forward_copy(k).start()

    send_back(middle, ROWS)

    own[...] += back_slice(0)
    for k in range(1, COLS + 1):
        forward_copy(k).wait_recv()
        own[...] += rrecv[k]
    for j in range(1, ROWS):
        back_copy(j).wait_recv()
        own[...] += brecv[j]
    img24[...] = own[...] * (LN2 * LN2 / 3.0 / 2.0**BOOST) + noise[...] * dir24[...]

    zeros8 = jnp.zeros((8, PTS), F32)
    zeros64 = jnp.zeros((64, PTS), F32)
    img, dirs, res = img24[...], dir24[...], res24[...]
    table = jnp.concatenate([dirs, zeros8, img, zeros8, zeros64], 0)
    other = jnp.concatenate([zeros64, img, zeros8, dirs, zeros8], 0)
    gram[...] = exact_dot(img, table, ((1,), (1,))) + exact_dot(res, other, ((1,), (1,)))

    def ar1_copy(j):
        return pltpu.make_async_remote_copy(
            src_ref=gram, dst_ref=ar1.at[m], send_sem=ar1_send.at[j], recv_sem=ar1_recv.at[j],
            device_id=row_peer(j), device_id_type=MESH)

    for j in range(1, ROWS):
        ar1_copy(j).start()
    ar1[m] = gram[...]
    for j in range(1, ROWS):
        ar1_copy(j).wait()
    total = ar1[0]
    for j in range(1, ROWS):
        total = total + ar1[j]
    gram[...] = total

    place = x * SIDE + z

    def ar2_copy(k):
        dx, dz = others[k]
        return pltpu.make_async_remote_copy(
            src_ref=gram, dst_ref=ar2.at[place], send_sem=ar2_send.at[k], recv_sem=ar2_recv.at[k],
            device_id=plane_peer(dx, dz), device_id_type=MESH)

    for k in range(PLANE - 1):
        ar2_copy(k).start()
    ar2[place] = gram[...]
    for k in range(PLANE - 1):
        ar2_copy(k).wait()
    total = ar2[0]
    for k in range(1, PLANE):
        total = total + ar2[k]

    curv = total[:, 0:SIDES_PAD]
    curv = 0.5 * (curv + curv.T)
    outer = pltpu.roll(total, 96, 1)[:, 0:SIDES_PAD]
    img_res = pltpu.roll(total, 64, 1)[:, 0:SIDES_PAD]
    dir_res = pltpu.roll(total, 32, 1)[:, 0:SIDES_PAD]
    row = lax.broadcasted_iota(jnp.int32, (SIDES_PAD, SIDES_PAD), 0)
    col = lax.broadcasted_iota(jnp.int32, (SIDES_PAD, SIDES_PAD), 1)
    inverse = (row == col).astype(F32)
    for i in range(SIDES):
        pivot = 1.0 / curv[i:i + 1, i:i + 1]
        head = curv[i:i + 1, :] * pivot
        tail = inverse[i:i + 1, :] * pivot
        factor = jnp.where(row[:, 0:1] == i, 0.0, curv[:, i:i + 1])
        curv = jnp.where(row == i, head, curv - factor * head)
        inverse = jnp.where(row == i, tail, inverse - factor * tail)

    step_t = exact_dot(dir_res, inverse)
    conj_t = exact_dot(exact_dot(step_t, outer) - img_res, inverse)
    res_new = res - exact_dot(step_t, img)
    new_solution[...] = solution[...] + exact_dot(step_t, dirs)[0:SIDES, :]
    new_residual[...] = res_new[0:SIDES, :]
    new_direction[...] = (res_new + exact_dot(conj_t, dirs))[0:SIDES, :]

    for j in range(1, ROWS):
        gather_copy(j).wait_send()
        back_copy(j).wait_send()
    for k in range(1, COLS + 1):
        column_copy(k).wait_send()
        forward_copy(k).wait_send()


def on_device(points, lengthscale, noise, solution, residual, direction):
    scale = (math.sqrt(5.0) / LN2 / lengthscale)[:, None]
    vmem = pl.BlockSpec(memory_space=pltpu.VMEM)
    sem = pltpu.SemaphoreType.DMA
    rows = ROWS * PTS
    return pl.pallas_call(
        kernel,
        out_shape=[jax.ShapeDtypeStruct((SIDES, PTS), F32)] * 3,
        in_specs=[vmem] * 6,
        out_specs=[vmem] * 3,
        scratch_shapes=[
            pltpu.VMEM((PACKET, PTS), F32),
            pltpu.VMEM((ROWS, PACKET, PTS), F32),
            pltpu.VMEM((COLS + 1, PACKET, PTS), F32),
            pltpu.VMEM((rows, DEPTH), BF16),
            pltpu.VMEM((2 * SIDES_PAD, rows), BF16),
            pltpu.VMEM((LOW, rows), F32),
            pltpu.VMEM((LOW, rows), F8),
            pltpu.VMEM((LOW, LANES), F32),
            pltpu.VMEM((DEPTH, PTS), BF16),
            pltpu.VMEM((PTS, LANES), BF16),
            pltpu.VMEM((PTS, LANES), F8),
            pltpu.VMEM((8, LANES), F32),
            pltpu.VMEM((COLS + 1, 2 * SIDES_PAD, PTS), F32),
            pltpu.VMEM((rows, LANES), F32),
            pltpu.VMEM((COLS + 1, SIDES_PAD, PTS), F32),
            pltpu.VMEM((COLS + 1, SIDES_PAD, PTS), F32),
            pltpu.VMEM((ROWS, SIDES_PAD, PTS), F32),
            pltpu.VMEM((ROWS, SIDES_PAD, PTS), F32),
            pltpu.VMEM((SIDES_PAD, PTS), F32),
            pltpu.VMEM((SIDES_PAD, PTS), F32),
            pltpu.VMEM((SIDES_PAD, PTS), F32),
            pltpu.VMEM((SIDES_PAD, 128), F32),
            pltpu.VMEM((ROWS, SIDES_PAD, 128), F32),
            pltpu.VMEM((PLANE, SIDES_PAD, 128), F32),
            pltpu.VMEM((SIDES_PAD, PTS), F32),
            sem((ROWS,)), sem((ROWS,)), sem((COLS + 1,)), sem((COLS + 1,)),
            sem((COLS + 1,)), sem((COLS + 1,)), sem((ROWS,)), sem((ROWS,)),
            sem((ROWS,)), sem((ROWS,)), sem((PLANE,)), sem((PLANE,)),
        ],
        compiler_params=pltpu.CompilerParams(
            collective_id=0, has_side_effects=True, vmem_limit_bytes=56 * 2**20
        ),
        cost_estimate=pl.CostEstimate(flops=30_000_000_000, bytes_accessed=1_000_000, transcendentals=34_000_000),
        name="block_cg",
    )(points, scale, noise.reshape(1, 1), solution, residual, direction)


def solution(mesh):
    placed = P(None, ("blk", "narrow"))
    return jax.shard_map(
        on_device,
        mesh=mesh,
        in_specs=(placed, P(), P(), placed, placed, placed),
        out_specs=(placed, placed, placed),
        check_vma=False,
    )
```

```python
import functools
import math

import jax
import jax.numpy as jnp
from jax import lax
from jax.experimental import pallas as pl
from jax.experimental.pallas import tpu as pltpu
from jax.sharding import PartitionSpec as P

BF16 = jnp.bfloat16
F32 = jnp.float32
LN2 = math.log(2.0)
MESH = pl.DeviceIdType.MESH
FEATS = 32
SIDES = 17
SIDES_PAD = 24
PTS = 512
ROWS = 8
PLANE = 16
SIDE = 4
FULL = 6
OFFSETS = ((1, 0), (0, 3), (1, 1), (3, 1), (2, 3), (3, 2), (2, 0), (0, 2), (2, 2))
COLS = len(OFFSETS)
STEP_X = tuple(dx for dx, _ in OFFSETS)
STEP_Z = tuple(dz for _, dz in OFFSETS)
PACKET = 49
DEPTH = 256
CHUNK = 2048
LANES = 128
LOW = 64
BOOST = 14
F8 = jnp.float8_e4m3fn
F8_TOP = 256.0


def dot(left, right, dims=((1,), (0,))):
    return lax.dot_general(left, right, (dims, ((), ())), preferred_element_type=F32)


def exact_dot(left, right, dims=((1,), (0,))):
    return lax.dot_general(
        left, right, (dims, ((), ())), precision=lax.Precision.HIGHEST, preferred_element_type=F32
    )


def split3(x):
    first = x.astype(BF16).astype(F32)
    second = (x - first).astype(BF16).astype(F32)
    third = (x - first - second).astype(BF16).astype(F32)
    return first, second, third


def norm_rows(squares, norms_first):
    s1, s2, s3 = split3(squares)
    row = lax.broadcasted_iota(jnp.int32, (16, PTS), 0)
    zero = jnp.zeros((16, PTS), F32)
    base = 0 if norms_first else 3
    ones = 3 if norms_first else 0
    out = jnp.where((row >= ones) & (row < ones + 3), 1.0, zero)
    for place, part in enumerate((s1, s2, s3)):
        out = jnp.where(row == base + place, jnp.broadcast_to(part, (16, PTS)), out)
    return out


def expand(pts, left):
    p1, p2, p3 = split3(pts)
    squares = jnp.sum(pts * pts, 0, keepdims=True)
    order = (p1, p1, p2, p2, p1, p3) if left else (p1, p2, p1, p2, p3, p1)
    scale = -2.0 if left else 1.0
    rows = [part * scale for part in order]
    rows.append(norm_rows(squares, left))
    rows.append(jnp.zeros((DEPTH - 6 * FEATS - 16, PTS), F32))
    return jnp.concatenate(rows, 0)


def split_dir(rows):
    hi = rows.astype(BF16).astype(F32)
    return jnp.concatenate([hi, rows - hi], 0).astype(BF16)


def matern(q):
    q = jnp.maximum(q, 1e-30)
    t = q * lax.rsqrt(q)
    return ((q + 3.0 / LN2**2) + t * (3.0 / LN2)) * jnp.exp2(BOOST - t)


def pick(k, values):
    if isinstance(k, int):
        return values[k - 1]
    out = values[0]
    for place, value in enumerate(values[1:], 2):
        out = jnp.where(k == place, value, out)
    return out


def kernel(points, scale, noise, solution, residual, direction, new_solution, new_residual, new_direction,
           pkt, gat, cols, left, ldir, ldirf, ldir8, lscale, right, rdir, rdir8, rscale, side24, fwds, back, rsend, rrecv, bsend, brecv, dir24, res24, img24,
           gram, ar1, ar2, own, tot24,
           gat_send, gat_recv, col_send, col_recv, r_send, r_recv, b_send, b_recv,
           ar1_send, ar1_recv, ar2_send, ar2_recv):
    b = lax.axis_index("blk")
    n = lax.axis_index("narrow")

    x = b // 8 * 2 + n % 2
    z = b // 2 % SIDE
    m = n // 2 * 2 + b % 2

    def device(x, z, m):
        return (x // 2 * 8 + z * 2 + m % 2, m // 2 * 2 + x % 2)

    def row_peer(j):
        return device(x, z, lax.rem(m + j, ROWS))

    def plane_peer(dx, dz):
        return device(lax.rem(x + dx, SIDE), lax.rem(z + dz, SIDE), m)

    others = [(dx, dz) for dx in range(SIDE) for dz in range(SIDE) if dx or dz]

    barrier = pltpu.get_barrier_semaphore()
    for j in range(1, ROWS):
        pl.semaphore_signal(barrier, inc=1, device_id=row_peer(j), device_id_type=MESH)
    for dx, dz in others:
        pl.semaphore_signal(barrier, inc=1, device_id=plane_peer(dx, dz), device_id_type=MESH)

    dir24[...] = jnp.zeros_like(dir24)
    dir24[0:SIDES, :] = direction[...]
    res24[...] = jnp.zeros_like(res24)
    res24[0:SIDES, :] = residual[...]
    pkt[0:FEATS, :] = points[...] * scale[...]
    pkt[FEATS:PACKET, :] = direction[...]
    side24[...] = jnp.zeros_like(side24)
    pl.semaphore_wait(barrier, ROWS + PLANE - 2)

    def gather_copy(j):
        return pltpu.make_async_remote_copy(
            src_ref=pkt, dst_ref=gat.at[j], send_sem=gat_send.at[j], recv_sem=gat_recv.at[j],
            device_id=row_peer(ROWS - j), device_id_type=MESH)

    def column_copy(k):
        return pltpu.make_async_remote_copy(
            src_ref=pkt, dst_ref=cols.at[k], send_sem=col_send.at[k], recv_sem=col_recv.at[k],
            device_id=plane_peer(SIDE - pick(k, STEP_X), SIDE - pick(k, STEP_Z)), device_id_type=MESH)

    def forward_copy(k):
        return pltpu.make_async_remote_copy(
            src_ref=rsend.at[k], dst_ref=rrecv.at[k], send_sem=r_send.at[k], recv_sem=r_recv.at[k],
            device_id=plane_peer(pick(k, STEP_X), pick(k, STEP_Z)), device_id_type=MESH)

    def back_copy(j):
        return pltpu.make_async_remote_copy(
            src_ref=bsend.at[j], dst_ref=brecv.at[j], send_sem=b_send.at[j], recv_sem=b_recv.at[j],
            device_id=row_peer(j), device_id_type=MESH)

    middle = ROWS // 2
    for j in range(1, middle):
        gather_copy(j).start()
    for k in range(1, COLS + 1):
        column_copy(k).start()

    def padded_sides(packet):
        side24[0:SIDES, :] = packet[FEATS:PACKET, :]
        return side24[...]

    def low_terms(rows, top):
        scaled = rows * (F8_TOP / top)
        first = scaled.astype(F8).astype(F32)
        return first, scaled - first

    def load_right(k, packet):
        right[k] = expand(packet[0:FEATS, :], False).astype(BF16)
        rows = padded_sides(packet)
        hi = rows.astype(BF16).astype(F32)
        top = jnp.maximum(jnp.max(jnp.abs(rows), 1, keepdims=True), 1e-30)
        first, second = low_terms(rows, top)
        scale_rows = jnp.broadcast_to(top * (1.0 / F8_TOP), rows.shape)
        spare = jnp.zeros((LANES - 5 * SIDES_PAD, PTS), F32)
        turned = jnp.concatenate([hi, rows - hi, first, second, scale_rows, spare], 0).T
        lane = lax.broadcasted_iota(jnp.int32, (PTS, LANES), 1)
        rdir[k] = jnp.where(lane < 2 * SIDES_PAD, turned, 0.0).astype(BF16)
        low = (lane >= 2 * SIDES_PAD) & (lane < 4 * SIDES_PAD)
        rdir8[k] = jnp.where(low, turned, 0.0).astype(F8)
        line = turned[0:8, :]
        near = pltpu.roll(line, LANES - SIDES_PAD, 1)
        far = pltpu.roll(line, LANES - 2 * SIDES_PAD, 1)
        rscale[k] = jnp.where(lane[0:8, :] < 3 * SIDES_PAD, far, near)

    def scale_left(half, at):
        rows = ldirf[:, at]
        top = jnp.maximum(jnp.max(jnp.abs(rows), 1, keepdims=True), 1e-30)
        first, second = low_terms(rows, top)
        spare = jnp.zeros((LOW - 2 * SIDES_PAD, rows.shape[1]), F32)
        ldir8[:, at] = jnp.concatenate([first, second, spare], 0).astype(F8)
        lscale[half] = jnp.broadcast_to(top * (1.0 / F8_TOP), (SIDES_PAD, LANES))

    def load_left(j, packet):
        at = pl.ds(pl.multiple_of(j * PTS, PTS), PTS)
        left[at, :] = expand(packet[0:FEATS, :], True).T.astype(BF16)
        rows = padded_sides(packet)
        ldir[:, at] = split_dir(rows)
        ldirf[:, at] = rows

    def tile(k, start, half, both):
        at = pl.ds(pl.multiple_of(start, PTS), CHUNK)
        kern = matern(dot(left[at, :], right[k]))
        hi = kern.astype(BF16)
        lo = (kern - hi.astype(F32)).astype(F8)
        if both:
            back[at, :] += dot(hi, rdir[k])
            back[at, :] += dot(lo, rdir8[k]) * rscale[k, 0:1]
        fwds[k] += dot(ldir[:, at], hi)
        low = dot(ldir8[:, at], lo)
        fwds[k, 0:SIDES_PAD] += (low[0:SIDES_PAD] + low[SIDES_PAD:2 * SIDES_PAD]) * lscale[half, :, 0:1]

    back[...] = jnp.zeros_like(back)
    fwds[...] = jnp.zeros_like(fwds)
    right[0] = expand(pkt[0:FEATS, :], False).astype(BF16)
    load_left(0, pkt)

    @pl.loop(1, middle)
    def _(j):
        gather_copy(j).wait_recv()
        load_left(j, gat.at[j])

    scale_left(0, pl.ds(0, middle * PTS))
    upper_x = jnp.where(x >= SIDE // 2, PTS, 0)
    upper_z = jnp.where(z >= SIDE // 2, PTS, 0)

    def back_slice(j):
        part = back[pl.ds(pl.multiple_of(j * PTS, PTS), PTS), :].T
        return sum(part[i * SIDES_PAD:i * SIDES_PAD + SIDES, :] for i in range(4))

    def send_back(first, last):
        @pl.loop(first, last)
        def _(j):
            bsend[j] = back_slice(j)
            back_copy(j).start()

    @pl.loop(0, COLS + FULL)
    def _(s):
        first = s < COLS
        k = jnp.where(first, s + 1, COLS + FULL - s)

        @pl.when(first)
        def _():
            column_copy(k).wait_recv()
            load_right(k, cols.at[k])

        @pl.when(s < ROWS - middle)
        def _():
            gather_copy(s + middle).start()

        @pl.when(s == FULL)
        def _():
            gather_copy(middle).wait_recv()
            load_left(middle, gat.at[middle])
            scale_left(0, pl.ds(0, (middle + 1) * PTS))

        @pl.when(s == COLS)
        def _():
            @pl.loop(middle + 1, ROWS)
            def _(j):
                gather_copy(j).wait_recv()
                load_left(j, gat.at[j])

            scale_left(1, pl.ds(middle * PTS, (ROWS - middle) * PTS))
            send_back(1, middle)

        upper = jnp.where(k == FULL + 2, upper_z, upper_x)
        tile(k, jnp.where(first, jnp.where(k > FULL, upper, 0), CHUNK), jnp.where(first, 0, 1), True)

        @pl.when(s >= FULL)
        def _():
            rsend[k] = fwds[k, 0:SIDES] + fwds[k, SIDES_PAD:SIDES_PAD + SIDES]
            forward_copy(k).start()

    send_back(middle, ROWS)

    @pl.loop(0, 2)
    def _(half):
        tile(0, half * CHUNK, half, False)

    own[...] = fwds[0, 0:SIDES_PAD] + fwds[0, SIDES_PAD:]
    own[0:SIDES, :] += back_slice(0)
    for k in range(1, COLS + 1):
        forward_copy(k).wait_recv()
        own[0:SIDES, :] += rrecv[k]
    for j in range(1, ROWS):
        back_copy(j).wait_recv()
        own[0:SIDES, :] += brecv[j]
    img24[...] = own[...] * (LN2 * LN2 / 3.0 / 2.0**BOOST) + noise[...] * dir24[...]

    zeros8 = jnp.zeros((8, PTS), F32)
    zeros64 = jnp.zeros((64, PTS), F32)
    img, dirs, res = img24[...], dir24[...], res24[...]
    table = jnp.concatenate([dirs, zeros8, img, zeros8, zeros64], 0)
    other = jnp.concatenate([zeros64, img, zeros8, dirs, zeros8], 0)
    gram[...] = (exact_dot(img, table, ((1,), (1,))) + exact_dot(res, other, ((1,), (1,))))[0:SIDES, :]

    def ar1_copy(j):
        return pltpu.make_async_remote_copy(
            src_ref=gram, dst_ref=ar1.at[m], send_sem=ar1_send.at[j], recv_sem=ar1_recv.at[j],
            device_id=row_peer(j), device_id_type=MESH)

    for j in range(1, ROWS):
        ar1_copy(j).start()
    ar1[m] = gram[...]
    for j in range(1, ROWS):
        ar1_copy(j).wait()
    total = ar1[0]
    for j in range(1, ROWS):
        total = total + ar1[j]
    gram[...] = total

    place = x * SIDE + z

    def ar2_copy(k):
        dx, dz = others[k]
        return pltpu.make_async_remote_copy(
            src_ref=gram, dst_ref=ar2.at[place], send_sem=ar2_send.at[k], recv_sem=ar2_recv.at[k],
            device_id=plane_peer(dx, dz), device_id_type=MESH)

    for k in range(PLANE - 1):
        ar2_copy(k).start()
    ar2[place] = gram[...]
    for k in range(PLANE - 1):
        ar2_copy(k).wait()
    total = ar2[0]
    for k in range(1, PLANE):
        total = total + ar2[k]

    tot24[...] = jnp.zeros_like(tot24)
    tot24[0:SIDES, :] = total
    total = tot24[...]
    curv = total[:, 0:SIDES_PAD]
    curv = 0.5 * (curv + curv.T)
    outer = pltpu.roll(total, 96, 1)[:, 0:SIDES_PAD]
    img_res = pltpu.roll(total, 64, 1)[:, 0:SIDES_PAD]
    dir_res = pltpu.roll(total, 32, 1)[:, 0:SIDES_PAD]
    row = lax.broadcasted_iota(jnp.int32, (SIDES_PAD, SIDES_PAD), 0)
    col = lax.broadcasted_iota(jnp.int32, (SIDES_PAD, SIDES_PAD), 1)
    inverse = (row == col).astype(F32)
    for i in range(SIDES):
        pivot = 1.0 / curv[i:i + 1, i:i + 1]
        head = curv[i:i + 1, :] * pivot
        tail = inverse[i:i + 1, :] * pivot
        factor = jnp.where(row[:, 0:1] == i, 0.0, curv[:, i:i + 1])
        curv = jnp.where(row == i, head, curv - factor * head)
        inverse = jnp.where(row == i, tail, inverse - factor * tail)

    step_t = exact_dot(dir_res, inverse)
    conj_t = exact_dot(exact_dot(step_t, outer) - img_res, inverse)
    res_new = res - exact_dot(step_t, img)
    new_solution[...] = solution[...] + exact_dot(step_t, dirs)[0:SIDES, :]
    new_residual[...] = res_new[0:SIDES, :]
    new_direction[...] = (res_new + exact_dot(conj_t, dirs))[0:SIDES, :]

    for j in range(1, ROWS):
        gather_copy(j).wait_send()
        back_copy(j).wait_send()
    for k in range(1, COLS + 1):
        column_copy(k).wait_send()
        forward_copy(k).wait_send()


def on_device(points, lengthscale, noise, solution, residual, direction):
    scale = (math.sqrt(5.0) / LN2 / lengthscale)[:, None]
    vmem = pl.BlockSpec(memory_space=pltpu.VMEM)
    sem = pltpu.SemaphoreType.DMA
    rows = ROWS * PTS
    return pl.pallas_call(
        kernel,
        out_shape=[jax.ShapeDtypeStruct((SIDES, PTS), F32)] * 3,
        in_specs=[vmem] * 6,
        out_specs=[vmem] * 3,
        scratch_shapes=[
            pltpu.VMEM((PACKET, PTS), F32),
            pltpu.VMEM((ROWS, PACKET, PTS), F32),
            pltpu.VMEM((COLS + 1, PACKET, PTS), F32),
            pltpu.VMEM((rows, DEPTH), BF16),
            pltpu.VMEM((2 * SIDES_PAD, rows), BF16),
            pltpu.VMEM((SIDES_PAD, rows), F32),
            pltpu.VMEM((LOW, rows), F8),
            pltpu.VMEM((2, SIDES_PAD, LANES), F32),
            pltpu.VMEM((COLS + 1, DEPTH, PTS), BF16),
            pltpu.VMEM((COLS + 1, PTS, LANES), BF16),
            pltpu.VMEM((COLS + 1, PTS, LANES), F8),
            pltpu.VMEM((COLS + 1, 8, LANES), F32),
            pltpu.VMEM((SIDES_PAD, PTS), F32),
            pltpu.VMEM((COLS + 1, 2 * SIDES_PAD, PTS), F32),
            pltpu.VMEM((rows, LANES), F32),
            pltpu.VMEM((COLS + 1, SIDES, PTS), F32),
            pltpu.VMEM((COLS + 1, SIDES, PTS), F32),
            pltpu.VMEM((ROWS, SIDES, PTS), F32),
            pltpu.VMEM((ROWS, SIDES, PTS), F32),
            pltpu.VMEM((SIDES_PAD, PTS), F32),
            pltpu.VMEM((SIDES_PAD, PTS), F32),
            pltpu.VMEM((SIDES_PAD, PTS), F32),
            pltpu.VMEM((SIDES, LANES), F32),
            pltpu.VMEM((ROWS, SIDES, LANES), F32),
            pltpu.VMEM((PLANE, SIDES, LANES), F32),
            pltpu.VMEM((SIDES_PAD, PTS), F32),
            pltpu.VMEM((SIDES_PAD, LANES), F32),
            sem((ROWS,)), sem((ROWS,)), sem((COLS + 1,)), sem((COLS + 1,)),
            sem((COLS + 1,)), sem((COLS + 1,)), sem((ROWS,)), sem((ROWS,)),
            sem((ROWS,)), sem((ROWS,)), sem((PLANE,)), sem((PLANE,)),
        ],
        compiler_params=pltpu.CompilerParams(
            collective_id=0, has_side_effects=True, vmem_limit_bytes=56 * 2**20
        ),
        cost_estimate=pl.CostEstimate(flops=30_000_000_000, bytes_accessed=1_000_000, transcendentals=34_000_000),
        name="block_cg",
    )(points, scale, noise.reshape(1, 1), solution, residual, direction)


def solution(mesh):
    placed = P(None, ("blk", "narrow"))
    return jax.shard_map(
        on_device,
        mesh=mesh,
        in_specs=(placed, P(), P(), placed, placed, placed),
        out_specs=(placed, placed, placed),
        check_vma=False,
    )
```

```python
import functools
import math

import jax
import jax.numpy as jnp
from jax import lax
from jax.experimental import pallas as pl
from jax.experimental.pallas import tpu as pltpu
from jax.sharding import PartitionSpec as P

BF16 = jnp.bfloat16
F32 = jnp.float32
LN2 = math.log(2.0)
MESH = pl.DeviceIdType.MESH
FEATS = 32
SIDES = 17
SIDES_PAD = 24
PTS = 512
ROWS = 8
PLANE = 16
SIDE = 4
FULL = 6
OFFSETS = ((1, 0), (0, 3), (1, 1), (3, 1), (2, 3), (3, 2), (2, 0), (0, 2), (2, 2))
COLS = len(OFFSETS)
ROW_OFFSETS = ((0, 0), (0, 1), (1, 0), (3, 1), (2, 0), (2, 1), (1, 1), (3, 0))
ROW_Y = tuple(dy for dy, _ in ROW_OFFSETS[1:])
ROW_C = tuple(dc for _, dc in ROW_OFFSETS[1:])
STEP_X = tuple(dx for dx, _ in OFFSETS)
STEP_Z = tuple(dz for _, dz in OFFSETS)
PACKET = 49
DEPTH = 256
CHUNK = 2048
LANES = 128
LOW = 64
BOOST = 14
F8 = jnp.float8_e4m3fn
F8_TOP = 256.0


def dot(left, right, dims=((1,), (0,))):
    return lax.dot_general(left, right, (dims, ((), ())), preferred_element_type=F32)


def exact_dot(left, right, dims=((1,), (0,))):
    return lax.dot_general(
        left, right, (dims, ((), ())), precision=lax.Precision.HIGHEST, preferred_element_type=F32
    )


def split3(x):
    first = x.astype(BF16).astype(F32)
    second = (x - first).astype(BF16).astype(F32)
    third = (x - first - second).astype(BF16).astype(F32)
    return first, second, third


def norm_rows(squares, norms_first):
    s1, s2, s3 = split3(squares)
    row = lax.broadcasted_iota(jnp.int32, (16, PTS), 0)
    zero = jnp.zeros((16, PTS), F32)
    base = 0 if norms_first else 3
    ones = 3 if norms_first else 0
    out = jnp.where((row >= ones) & (row < ones + 3), 1.0, zero)
    for place, part in enumerate((s1, s2, s3)):
        out = jnp.where(row == base + place, jnp.broadcast_to(part, (16, PTS)), out)
    return out


def expand(pts, left):
    p1, p2, p3 = split3(pts)
    squares = jnp.sum(pts * pts, 0, keepdims=True)
    order = (p1, p1, p2, p2, p1, p3) if left else (p1, p2, p1, p2, p3, p1)
    scale = -2.0 if left else 1.0
    rows = [part * scale for part in order]
    rows.append(norm_rows(squares, left))
    rows.append(jnp.zeros((DEPTH - 6 * FEATS - 16, PTS), F32))
    return jnp.concatenate(rows, 0)


def split_dir(rows):
    hi = rows.astype(BF16).astype(F32)
    return jnp.concatenate([hi, rows - hi], 0).astype(BF16)


def matern(q):
    q = jnp.maximum(q, 1e-30)
    t = q * lax.rsqrt(q)
    return ((q + 3.0 / LN2**2) + t * (3.0 / LN2)) * jnp.exp2(BOOST - t)


def pick(k, values):
    if isinstance(k, int):
        return values[k - 1]
    out = values[0]
    for place, value in enumerate(values[1:], 2):
        out = jnp.where(k == place, value, out)
    return out


def kernel(points, scale, noise, residual, direction, img24, total_out,
           pkt, gat, cols, left, ldir, ldirf, ldir8, lscale, right, rdir, rdir8, rscale, side24, fwds, back, rsend, rrecv, bsend, brecv, dir24, res24,
           gram, ar1, ar2, own,
           gat_send, gat_recv, col_send, col_recv, r_send, r_recv, b_send, b_recv,
           ar1_send, ar1_recv, ar2_send, ar2_recv):
    b = lax.axis_index("blk")
    n = lax.axis_index("narrow")

    x = b // 8 * 2 + n % 2
    z = b // 2 % SIDE
    y = n // 2
    c = b % 2
    m = y * 2 + c

    def device(x, z, y, c):
        return (x // 2 * 8 + z * 2 + c, y * 2 + x % 2)

    def row_peer(dy, dc):
        return device(x, z, lax.rem(y + dy, SIDE), lax.rem(c + dc, 2))

    def plane_peer(dx, dz):
        return device(lax.rem(x + dx, SIDE), lax.rem(z + dz, SIDE), y, c)

    others = [(dx, dz) for dx in range(SIDE) for dz in range(SIDE) if dx or dz]

    barrier = pltpu.get_barrier_semaphore()
    for j in range(1, ROWS):
        pl.semaphore_signal(barrier, inc=1, device_id=row_peer(pick(j, ROW_Y), pick(j, ROW_C)), device_id_type=MESH)
    for dx, dz in others:
        pl.semaphore_signal(barrier, inc=1, device_id=plane_peer(dx, dz), device_id_type=MESH)

    dir24[...] = jnp.zeros_like(dir24)
    dir24[0:SIDES, :] = direction[...]
    res24[...] = jnp.zeros_like(res24)
    res24[0:SIDES, :] = residual[...]
    pkt[0:FEATS, :] = points[...] * scale[...]
    pkt[FEATS:PACKET, :] = direction[...]
    side24[...] = jnp.zeros_like(side24)
    pl.semaphore_wait(barrier, ROWS + PLANE - 2)

    def gather_copy(j):
        return pltpu.make_async_remote_copy(
            src_ref=pkt, dst_ref=gat.at[j], send_sem=gat_send.at[j], recv_sem=gat_recv.at[j],
            device_id=row_peer(SIDE - pick(j, ROW_Y), pick(j, ROW_C)), device_id_type=MESH)

    def column_copy(k):
        return pltpu.make_async_remote_copy(
            src_ref=pkt, dst_ref=cols.at[k], send_sem=col_send.at[k], recv_sem=col_recv.at[k],
            device_id=plane_peer(SIDE - pick(k, STEP_X), SIDE - pick(k, STEP_Z)), device_id_type=MESH)

    def forward_copy(k):
        return pltpu.make_async_remote_copy(
            src_ref=rsend.at[k], dst_ref=rrecv.at[k], send_sem=r_send.at[k], recv_sem=r_recv.at[k],
            device_id=plane_peer(pick(k, STEP_X), pick(k, STEP_Z)), device_id_type=MESH)

    def back_copy(j):
        return pltpu.make_async_remote_copy(
            src_ref=bsend.at[j], dst_ref=brecv.at[j], send_sem=b_send.at[j], recv_sem=b_recv.at[j],
            device_id=row_peer(pick(j, ROW_Y), pick(j, ROW_C)), device_id_type=MESH)

    middle = ROWS // 2
    for j in range(1, middle):
        gather_copy(j).start()
    for k in range(1, COLS + 1):
        column_copy(k).start()

    def padded_sides(packet):
        side24[0:SIDES, :] = packet[FEATS:PACKET, :]
        return side24[...]

    def low_terms(rows, top):
        scaled = rows * (F8_TOP / top)
        first = scaled.astype(F8).astype(F32)
        return first, scaled - first

    def load_right(k, packet):
        right[k] = expand(packet[0:FEATS, :], False).astype(BF16)
        rows = padded_sides(packet)
        hi = rows.astype(BF16).astype(F32)
        top = jnp.maximum(jnp.max(jnp.abs(rows), 1, keepdims=True), 1e-30)
        first, second = low_terms(rows, top)
        scale_rows = jnp.broadcast_to(top * (1.0 / F8_TOP), rows.shape)
        spare = jnp.zeros((LANES - 5 * SIDES_PAD, PTS), F32)
        turned = jnp.concatenate([hi, rows - hi, first, second, scale_rows, spare], 0).T
        lane = lax.broadcasted_iota(jnp.int32, (PTS, LANES), 1)
        rdir[k] = jnp.where(lane < 2 * SIDES_PAD, turned, 0.0).astype(BF16)
        low = (lane >= 2 * SIDES_PAD) & (lane < 4 * SIDES_PAD)
        rdir8[k] = jnp.where(low, turned, 0.0).astype(F8)
        line = turned[0:8, :]
        near = pltpu.roll(line, LANES - SIDES_PAD, 1)
        far = pltpu.roll(line, LANES - 2 * SIDES_PAD, 1)
        rscale[k] = jnp.where(lane[0:8, :] < 3 * SIDES_PAD, far, near)

    def scale_left(half, at):
        rows = ldirf[:, at]
        top = jnp.maximum(jnp.max(jnp.abs(rows), 1, keepdims=True), 1e-30)
        first, second = low_terms(rows, top)
        spare = jnp.zeros((LOW - 2 * SIDES_PAD, rows.shape[1]), F32)
        ldir8[:, at] = jnp.concatenate([first, second, spare], 0).astype(F8)
        lscale[half] = jnp.broadcast_to(top * (1.0 / F8_TOP), (SIDES_PAD, LANES))

    def load_left(j, packet):
        at = pl.ds(pl.multiple_of(j * PTS, PTS), PTS)
        left[at, :] = expand(packet[0:FEATS, :], True).T.astype(BF16)
        rows = padded_sides(packet)
        ldir[:, at] = split_dir(rows)
        ldirf[:, at] = rows

    def tile(k, start, half, both):
        at = pl.ds(pl.multiple_of(start, PTS), CHUNK)
        kern = matern(dot(left[at, :], right[k]))
        hi = kern.astype(BF16)
        lo = (kern - hi.astype(F32)).astype(F8)
        if both:
            back[at, :] += dot(hi, rdir[k])
            back[at, :] += dot(lo, rdir8[k]) * rscale[k, 0:1]
        fwds[k] += dot(ldir[:, at], hi)
        low = dot(ldir8[:, at], lo)
        fwds[k, 0:SIDES_PAD] += (low[0:SIDES_PAD] + low[SIDES_PAD:2 * SIDES_PAD]) * lscale[half, :, 0:1]

    back[...] = jnp.zeros_like(back)
    fwds[...] = jnp.zeros_like(fwds)
    right[0] = expand(pkt[0:FEATS, :], False).astype(BF16)
    load_left(0, pkt)

    @pl.loop(1, middle)
    def _(j):
        gather_copy(j).wait_recv()
        load_left(j, gat.at[j])

    scale_left(0, pl.ds(0, middle * PTS))
    upper_x = jnp.where(x >= SIDE // 2, 2 * PTS, 0)
    upper_z = jnp.where(z >= SIDE // 2, 2 * PTS, 0)

    def back_slice(j):
        part = back[pl.ds(pl.multiple_of(j * PTS, PTS), PTS), :].T
        return sum(part[i * SIDES_PAD:i * SIDES_PAD + SIDES, :] for i in range(4))

    def send_back(first, last):
        @pl.loop(first, last)
        def _(j):
            bsend[j] = back_slice(j)
            back_copy(j).start()

    @pl.loop(0, COLS + FULL)
    def _(s):
        first = s < COLS
        k = jnp.where(first, s + 1, COLS + FULL - s)

        @pl.when(first)
        def _():
            column_copy(k).wait_recv()
            load_right(k, cols.at[k])

        @pl.when(s < ROWS - middle)
        def _():
            gather_copy(s + middle).start()

        @pl.when(s == FULL)
        def _():
            @pl.loop(middle, middle + 2)
            def _(j):
                gather_copy(j).wait_recv()
                load_left(j, gat.at[j])

            scale_left(0, pl.ds(0, (middle + 2) * PTS))

        @pl.when(s == COLS)
        def _():
            @pl.loop(middle + 2, ROWS)
            def _(j):
                gather_copy(j).wait_recv()
                load_left(j, gat.at[j])

            scale_left(1, pl.ds(middle * PTS, (ROWS - middle) * PTS))
            send_back(1, middle)

        upper = jnp.where(k == FULL + 2, upper_z, upper_x)
        tile(k, jnp.where(first, jnp.where(k > FULL, upper, 0), CHUNK), jnp.where(first, 0, 1), True)

        @pl.when(s >= FULL)
        def _():
            rsend[k] = fwds[k, 0:SIDES] + fwds[k, SIDES_PAD:SIDES_PAD + SIDES]
            forward_copy(k).start()

    send_back(middle, ROWS)

    @pl.loop(0, 2)
    def _(half):
        tile(0, half * CHUNK, half, False)

    own[...] = fwds[0, 0:SIDES_PAD] + fwds[0, SIDES_PAD:]
    own[0:SIDES, :] += back_slice(0)
    for k in range(1, COLS + 1):
        forward_copy(k).wait_recv()
        own[0:SIDES, :] += rrecv[k]
    for j in range(1, ROWS):
        back_copy(j).wait_recv()
        own[0:SIDES, :] += brecv[j]
    img24[...] = own[...] * (LN2 * LN2 / 3.0 / 2.0**BOOST) + noise[...] * dir24[...]

    zeros8 = jnp.zeros((8, PTS), F32)
    zeros64 = jnp.zeros((64, PTS), F32)
    img, dirs, res = img24[...], dir24[...], res24[...]
    table = jnp.concatenate([dirs, zeros8, img, zeros8, zeros64], 0)
    other = jnp.concatenate([zeros64, img, zeros8, dirs, zeros8], 0)
    gram[...] = (exact_dot(img, table, ((1,), (1,))) + exact_dot(res, other, ((1,), (1,))))[0:SIDES, :]

    def ar1_copy(j):
        return pltpu.make_async_remote_copy(
            src_ref=gram, dst_ref=ar1.at[m], send_sem=ar1_send.at[j], recv_sem=ar1_recv.at[j],
            device_id=row_peer(pick(j, ROW_Y), pick(j, ROW_C)), device_id_type=MESH)

    for j in range(1, ROWS):
        ar1_copy(j).start()
    ar1[m] = gram[...]
    for j in range(1, ROWS):
        ar1_copy(j).wait()
    total = ar1[0]
    for j in range(1, ROWS):
        total = total + ar1[j]
    gram[...] = total

    place = x * SIDE + z

    def ar2_copy(k):
        dx, dz = others[k]
        return pltpu.make_async_remote_copy(
            src_ref=gram, dst_ref=ar2.at[place], send_sem=ar2_send.at[k], recv_sem=ar2_recv.at[k],
            device_id=plane_peer(dx, dz), device_id_type=MESH)

    for k in range(PLANE - 1):
        ar2_copy(k).start()
    ar2[place] = gram[...]
    for k in range(PLANE - 1):
        ar2_copy(k).wait()
    total = ar2[0]
    for k in range(1, PLANE):
        total = total + ar2[k]

    total_out[...] = jnp.zeros_like(total_out)
    total_out[0:SIDES, :] = total

    for j in range(1, ROWS):
        gather_copy(j).wait_send()
        back_copy(j).wait_send()
    for k in range(1, COLS + 1):
        column_copy(k).wait_send()
        forward_copy(k).wait_send()


def solve_kernel(img24, total_in, solution, residual, direction, new_solution, new_residual, new_direction, dir24):
    total = total_in[...]
    img = img24[...]
    dir24[...] = jnp.zeros_like(dir24)
    dir24[0:SIDES, :] = direction[...]
    dirs = dir24[...]
    curv = total[:, 0:SIDES_PAD]
    curv = 0.5 * (curv + curv.T)
    outer = pltpu.roll(total, 96, 1)[:, 0:SIDES_PAD]
    img_res = pltpu.roll(total, 64, 1)[:, 0:SIDES_PAD]
    dir_res = pltpu.roll(total, 32, 1)[:, 0:SIDES_PAD]
    row = lax.broadcasted_iota(jnp.int32, (SIDES_PAD, SIDES_PAD), 0)
    col = lax.broadcasted_iota(jnp.int32, (SIDES_PAD, SIDES_PAD), 1)
    inverse = (row == col).astype(F32)
    for i in range(SIDES):
        pivot = 1.0 / curv[i:i + 1, i:i + 1]
        head = curv[i:i + 1, :] * pivot
        tail = inverse[i:i + 1, :] * pivot
        factor = jnp.where(row[:, 0:1] == i, 0.0, curv[:, i:i + 1])
        curv = jnp.where(row == i, head, curv - factor * head)
        inverse = jnp.where(row == i, tail, inverse - factor * tail)

    step_t = exact_dot(dir_res, inverse)
    conj_t = exact_dot(exact_dot(step_t, outer) - img_res, inverse)
    moved = exact_dot(step_t, img)
    new_solution[...] = solution[...] + exact_dot(step_t, dirs)[0:SIDES, :]
    res_new = residual[...] - moved[0:SIDES, :]
    new_residual[...] = res_new
    new_direction[...] = res_new + exact_dot(conj_t, dirs)[0:SIDES, :]


def on_device(points, lengthscale, noise, solution, residual, direction):
    scale = (math.sqrt(5.0) / LN2 / lengthscale)[:, None]
    vmem = pl.BlockSpec(memory_space=pltpu.VMEM)
    sem = pltpu.SemaphoreType.DMA
    rows = ROWS * PTS
    image, total = pl.pallas_call(
        kernel,
        out_shape=[jax.ShapeDtypeStruct((SIDES_PAD, PTS), F32), jax.ShapeDtypeStruct((SIDES_PAD, LANES), F32)],
        in_specs=[vmem] * 5,
        out_specs=[vmem] * 2,
        scratch_shapes=[
            pltpu.VMEM((PACKET, PTS), F32),
            pltpu.VMEM((ROWS, PACKET, PTS), F32),
            pltpu.VMEM((COLS + 1, PACKET, PTS), F32),
            pltpu.VMEM((rows, DEPTH), BF16),
            pltpu.VMEM((2 * SIDES_PAD, rows), BF16),
            pltpu.VMEM((SIDES_PAD, rows), F32),
            pltpu.VMEM((LOW, rows), F8),
            pltpu.VMEM((2, SIDES_PAD, LANES), F32),
            pltpu.VMEM((COLS + 1, DEPTH, PTS), BF16),
            pltpu.VMEM((COLS + 1, PTS, LANES), BF16),
            pltpu.VMEM((COLS + 1, PTS, LANES), F8),
            pltpu.VMEM((COLS + 1, 8, LANES), F32),
            pltpu.VMEM((SIDES_PAD, PTS), F32),
            pltpu.VMEM((COLS + 1, 2 * SIDES_PAD, PTS), F32),
            pltpu.VMEM((rows, LANES), F32),
            pltpu.VMEM((COLS + 1, SIDES, PTS), F32),
            pltpu.VMEM((COLS + 1, SIDES, PTS), F32),
            pltpu.VMEM((ROWS, SIDES, PTS), F32),
            pltpu.VMEM((ROWS, SIDES, PTS), F32),
            pltpu.VMEM((SIDES_PAD, PTS), F32),
            pltpu.VMEM((SIDES_PAD, PTS), F32),
            pltpu.VMEM((SIDES, LANES), F32),
            pltpu.VMEM((ROWS, SIDES, LANES), F32),
            pltpu.VMEM((PLANE, SIDES, LANES), F32),
            pltpu.VMEM((SIDES_PAD, PTS), F32),
            sem((ROWS,)), sem((ROWS,)), sem((COLS + 1,)), sem((COLS + 1,)),
            sem((COLS + 1,)), sem((COLS + 1,)), sem((ROWS,)), sem((ROWS,)),
            sem((ROWS,)), sem((ROWS,)), sem((PLANE,)), sem((PLANE,)),
        ],
        compiler_params=pltpu.CompilerParams(
            collective_id=0, has_side_effects=True, vmem_limit_bytes=56 * 2**20
        ),
        cost_estimate=pl.CostEstimate(flops=30_000_000_000, bytes_accessed=1_000_000, transcendentals=34_000_000),
        name="block_cg",
    )(points, scale, noise.reshape(1, 1), residual, direction)
    return pl.pallas_call(
        solve_kernel,
        out_shape=[jax.ShapeDtypeStruct((SIDES, PTS), F32)] * 3,
        in_specs=[vmem] * 5,
        out_specs=[vmem] * 3,
        scratch_shapes=[pltpu.VMEM((SIDES_PAD, PTS), F32)],
        name="solve",
    )(image, total, solution, residual, direction)


def solution(mesh):
    placed = P(None, ("blk", "narrow"))
    return jax.shard_map(
        on_device,
        mesh=mesh,
        in_specs=(placed, P(), P(), placed, placed, placed),
        out_specs=(placed, placed, placed),
        check_vma=False,
    )
```

```python
import functools
import math

import jax
import jax.numpy as jnp
from jax import lax
from jax.experimental import pallas as pl
from jax.experimental.pallas import tpu as pltpu
from jax.sharding import PartitionSpec as P

BF16 = jnp.bfloat16
F32 = jnp.float32
LN2 = math.log(2.0)
MESH = pl.DeviceIdType.MESH
FEATS = 32
SIDES = 17
SIDES_PAD = 24
PTS = 512
ROWS = 8
PLANE = 16
SIDE = 4
FULL = 6
OFFSETS = ((1, 0), (0, 3), (1, 1), (3, 1), (2, 3), (3, 2), (2, 0), (0, 2), (2, 2))
COLS = len(OFFSETS)
ROW_OFFSETS = ((0, 0), (0, 1), (1, 0), (3, 1), (2, 0), (2, 1), (1, 1), (3, 0))
ROW_Y = tuple(dy for dy, _ in ROW_OFFSETS[1:])
ROW_C = tuple(dc for _, dc in ROW_OFFSETS[1:])
STEP_X = tuple(dx for dx, _ in OFFSETS)
STEP_Z = tuple(dz for _, dz in OFFSETS)
PACKET = 49
DEPTH = 256
CHUNK = 2048
LANES = 128
LOW = 64
BOOST = 14
F8 = jnp.float8_e4m3fn
F8_TOP = 256.0


def dot(left, right, dims=((1,), (0,))):
    return lax.dot_general(left, right, (dims, ((), ())), preferred_element_type=F32)


def exact_dot(left, right, dims=((1,), (0,))):
    return lax.dot_general(
        left, right, (dims, ((), ())), precision=lax.Precision.HIGHEST, preferred_element_type=F32
    )


def split3(x):
    first = x.astype(BF16).astype(F32)
    second = (x - first).astype(BF16).astype(F32)
    third = (x - first - second).astype(BF16).astype(F32)
    return first, second, third


def norm_rows(squares, norms_first):
    s1, s2, s3 = split3(squares)
    row = lax.broadcasted_iota(jnp.int32, (16, PTS), 0)
    zero = jnp.zeros((16, PTS), F32)
    base = 0 if norms_first else 3
    ones = 3 if norms_first else 0
    out = jnp.where((row >= ones) & (row < ones + 3), 1.0, zero)
    for place, part in enumerate((s1, s2, s3)):
        out = jnp.where(row == base + place, jnp.broadcast_to(part, (16, PTS)), out)
    return out


def expand(pts, left):
    p1, p2, p3 = split3(pts)
    squares = jnp.sum(pts * pts, 0, keepdims=True)
    order = (p1, p1, p2, p2, p1, p3) if left else (p1, p2, p1, p2, p3, p1)
    scale = -2.0 if left else 1.0
    rows = [part * scale for part in order]
    rows.append(norm_rows(squares, left))
    rows.append(jnp.zeros((DEPTH - 6 * FEATS - 16, PTS), F32))
    return jnp.concatenate(rows, 0)


def split_dir(rows):
    hi = rows.astype(BF16).astype(F32)
    return jnp.concatenate([hi, rows - hi], 0).astype(BF16)


def matern(q):
    q = jnp.maximum(q, 1e-30)
    t = q * lax.rsqrt(q)
    return ((q + 3.0 / LN2**2) + t * (3.0 / LN2)) * jnp.exp2(BOOST - t)


def pick(k, values):
    if isinstance(k, int):
        return values[k - 1]
    out = values[0]
    for place, value in enumerate(values[1:], 2):
        out = jnp.where(k == place, value, out)
    return out


def kernel(points, lengthscale, noise, residual, direction, img24, total_out,
           pkt, gat, cols, left, ldir, ldirf, ldir8, lscale, right, rdir, rdir8, rscale, side24, fwds, back, rsend, rrecv, bsend, brecv, dir24, res24,
           gram, ar1, ar2, own,
           gat_send, gat_recv, col_send, col_recv, r_send, r_recv, b_send, b_recv,
           ar1_send, ar1_recv, ar2_send, ar2_recv):
    b = lax.axis_index("blk")
    n = lax.axis_index("narrow")

    x = b // 8 * 2 + n % 2
    z = b // 2 % SIDE
    y = n // 2
    c = b % 2
    m = y * 2 + c

    def device(x, z, y, c):
        return (x // 2 * 8 + z * 2 + c, y * 2 + x % 2)

    def row_peer(dy, dc):
        return device(x, z, lax.rem(y + dy, SIDE), lax.rem(c + dc, 2))

    def plane_peer(dx, dz):
        return device(lax.rem(x + dx, SIDE), lax.rem(z + dz, SIDE), y, c)

    others = [(dx, dz) for dx in range(SIDE) for dz in range(SIDE) if dx or dz]

    barrier = pltpu.get_barrier_semaphore()
    for j in range(1, ROWS):
        pl.semaphore_signal(barrier, inc=1, device_id=row_peer(pick(j, ROW_Y), pick(j, ROW_C)), device_id_type=MESH)
    for dx, dz in others:
        pl.semaphore_signal(barrier, inc=1, device_id=plane_peer(dx, dz), device_id_type=MESH)

    dir24[...] = jnp.zeros_like(dir24)
    dir24[0:SIDES, :] = direction[...]
    res24[...] = jnp.zeros_like(res24)
    res24[0:SIDES, :] = residual[...]
    diagonal = lax.broadcasted_iota(jnp.int32, (FEATS, FEATS), 0) == lax.broadcasted_iota(jnp.int32, (FEATS, FEATS), 1)
    lengths = jnp.sum(jnp.where(diagonal, jnp.broadcast_to(lengthscale[...], (FEATS, FEATS)), 0.0), 1, keepdims=True)
    pkt[0:FEATS, :] = points[...] * (math.sqrt(5.0) / LN2 / lengths)
    pkt[FEATS:PACKET, :] = direction[...]
    side24[...] = jnp.zeros_like(side24)
    pl.semaphore_wait(barrier, ROWS + PLANE - 2)

    def gather_copy(j):
        return pltpu.make_async_remote_copy(
            src_ref=pkt, dst_ref=gat.at[j], send_sem=gat_send.at[j], recv_sem=gat_recv.at[j],
            device_id=row_peer(SIDE - pick(j, ROW_Y), pick(j, ROW_C)), device_id_type=MESH)

    def column_copy(k):
        return pltpu.make_async_remote_copy(
            src_ref=pkt, dst_ref=cols.at[k], send_sem=col_send.at[k], recv_sem=col_recv.at[k],
            device_id=plane_peer(SIDE - pick(k, STEP_X), SIDE - pick(k, STEP_Z)), device_id_type=MESH)

    def forward_copy(k):
        return pltpu.make_async_remote_copy(
            src_ref=rsend.at[k], dst_ref=rrecv.at[k], send_sem=r_send.at[k], recv_sem=r_recv.at[k],
            device_id=plane_peer(pick(k, STEP_X), pick(k, STEP_Z)), device_id_type=MESH)

    def back_copy(j):
        return pltpu.make_async_remote_copy(
            src_ref=bsend.at[j], dst_ref=brecv.at[j], send_sem=b_send.at[j], recv_sem=b_recv.at[j],
            device_id=row_peer(pick(j, ROW_Y), pick(j, ROW_C)), device_id_type=MESH)

    middle = ROWS // 2
    for j in range(1, middle):
        gather_copy(j).start()
    for k in range(1, COLS + 1):
        column_copy(k).start()

    def padded_sides(packet):
        side24[0:SIDES, :] = packet[FEATS:PACKET, :]
        return side24[...]

    def low_terms(rows, top):
        scaled = rows * (F8_TOP / top)
        first = scaled.astype(F8).astype(F32)
        return first, scaled - first

    def load_right(k, packet):
        right[k] = expand(packet[0:FEATS, :], False).astype(BF16)
        rows = padded_sides(packet)
        hi = rows.astype(BF16).astype(F32)
        top = jnp.maximum(jnp.max(jnp.abs(rows), 1, keepdims=True), 1e-30)
        first, second = low_terms(rows, top)
        scale_rows = jnp.broadcast_to(top * (1.0 / F8_TOP), rows.shape)
        spare = jnp.zeros((LANES - 5 * SIDES_PAD, PTS), F32)
        turned = jnp.concatenate([hi, rows - hi, first, second, scale_rows, spare], 0).T
        lane = lax.broadcasted_iota(jnp.int32, (PTS, LANES), 1)
        rdir[k] = jnp.where(lane < 2 * SIDES_PAD, turned, 0.0).astype(BF16)
        low = (lane >= 2 * SIDES_PAD) & (lane < 4 * SIDES_PAD)
        rdir8[k] = jnp.where(low, turned, 0.0).astype(F8)
        line = turned[0:8, :]
        near = pltpu.roll(line, LANES - SIDES_PAD, 1)
        far = pltpu.roll(line, LANES - 2 * SIDES_PAD, 1)
        rscale[k] = jnp.where(lane[0:8, :] < 3 * SIDES_PAD, far, near)

    def scale_left(half, at):
        rows = ldirf[:, at]
        top = jnp.maximum(jnp.max(jnp.abs(rows), 1, keepdims=True), 1e-30)
        first, second = low_terms(rows, top)
        spare = jnp.zeros((LOW - 2 * SIDES_PAD, rows.shape[1]), F32)
        ldir8[:, at] = jnp.concatenate([first, second, spare], 0).astype(F8)
        lscale[half] = jnp.broadcast_to(top * (1.0 / F8_TOP), (SIDES_PAD, LANES))

    def load_left(j, packet):
        at = pl.ds(pl.multiple_of(j * PTS, PTS), PTS)
        left[at, :] = expand(packet[0:FEATS, :], True).T.astype(BF16)
        rows = padded_sides(packet)
        ldir[:, at] = split_dir(rows)
        ldirf[:, at] = rows

    def tile(k, start, half, both):
        at = pl.ds(pl.multiple_of(start, PTS), CHUNK)
        piece = 512
        waiting = None
        for place in range(0, CHUNK + piece, piece):
            fresh = None
            if place < CHUNK:
                at = pl.ds(pl.multiple_of(start + place, PTS), piece)
                kern = matern(dot(left[at, :], right[k]))
                hi = kern.astype(BF16)
                fresh = at, hi, (kern - hi.astype(F32)).astype(F8)
            if waiting is not None:
                at, hi, lo = waiting
                if both:
                    back[at, :] += dot(hi, rdir[k])
                    back[at, :] += dot(lo, rdir8[k]) * rscale[k, 0:1]
                fwds[k] += dot(ldir[:, at], hi)
                low = dot(ldir8[:, at], lo)
                fwds[k, 0:SIDES_PAD] += (low[0:SIDES_PAD] + low[SIDES_PAD:2 * SIDES_PAD]) * lscale[half, :, 0:1]
            waiting = fresh

    back[...] = jnp.zeros_like(back)
    fwds[...] = jnp.zeros_like(fwds)
    right[0] = expand(pkt[0:FEATS, :], False).astype(BF16)
    load_left(0, pkt)

    @pl.loop(1, middle)
    def _(j):
        gather_copy(j).wait_recv()
        load_left(j, gat.at[j])

    scale_left(0, pl.ds(0, middle * PTS))
    upper_x = jnp.where(x >= SIDE // 2, 2 * PTS, 0)
    upper_z = jnp.where(z >= SIDE // 2, 2 * PTS, 0)

    def back_slice(j):
        part = back[pl.ds(pl.multiple_of(j * PTS, PTS), PTS), :].T
        return sum(part[i * SIDES_PAD:i * SIDES_PAD + SIDES, :] for i in range(4))

    def send_back(first, last):
        @pl.loop(first, last)
        def _(j):
            bsend[j] = back_slice(j)
            back_copy(j).start()

    @pl.loop(0, COLS + FULL)
    def _(s):
        first = s < COLS
        k = jnp.where(first, s + 1, COLS + FULL - s)

        @pl.when(first)
        def _():
            column_copy(k).wait_recv()
            load_right(k, cols.at[k])

        @pl.when(s < ROWS - middle)
        def _():
            gather_copy(s + middle).start()

        @pl.when(s == FULL)
        def _():
            @pl.loop(middle, middle + 2)
            def _(j):
                gather_copy(j).wait_recv()
                load_left(j, gat.at[j])

            scale_left(0, pl.ds(0, (middle + 2) * PTS))

        @pl.when(s == COLS)
        def _():
            @pl.loop(middle + 2, ROWS)
            def _(j):
                gather_copy(j).wait_recv()
                load_left(j, gat.at[j])

            scale_left(1, pl.ds(middle * PTS, (ROWS - middle) * PTS))
            send_back(1, middle)

        upper = jnp.where(k == FULL + 2, upper_z, upper_x)
        tile(k, jnp.where(first, jnp.where(k > FULL, upper, 0), CHUNK), jnp.where(first, 0, 1), True)

        @pl.when(s >= FULL)
        def _():
            rsend[k] = fwds[k, 0:SIDES] + fwds[k, SIDES_PAD:SIDES_PAD + SIDES]
            forward_copy(k).start()

    send_back(middle, ROWS)

    @pl.loop(0, 2)
    def _(half):
        tile(0, half * CHUNK, half, False)

    own[...] = fwds[0, 0:SIDES_PAD] + fwds[0, SIDES_PAD:]
    own[0:SIDES, :] += back_slice(0)
    for k in range(1, COLS + 1):
        forward_copy(k).wait_recv()
        own[0:SIDES, :] += rrecv[k]
    for j in range(1, ROWS):
        back_copy(j).wait_recv()
        own[0:SIDES, :] += brecv[j]
    img24[...] = own[...] * (LN2 * LN2 / 3.0 / 2.0**BOOST) + noise[...] * dir24[...]

    zeros8 = jnp.zeros((8, PTS), F32)
    zeros64 = jnp.zeros((64, PTS), F32)
    img, dirs, res = img24[...], dir24[...], res24[...]
    table = jnp.concatenate([dirs, zeros8, img, zeros8, zeros64], 0)
    other = jnp.concatenate([zeros64, img, zeros8, dirs, zeros8], 0)
    gram[...] = (exact_dot(img, table, ((1,), (1,))) + exact_dot(res, other, ((1,), (1,))))[0:SIDES, :]

    def ar1_copy(j):
        return pltpu.make_async_remote_copy(
            src_ref=gram, dst_ref=ar1.at[m], send_sem=ar1_send.at[j], recv_sem=ar1_recv.at[j],
            device_id=row_peer(pick(j, ROW_Y), pick(j, ROW_C)), device_id_type=MESH)

    for j in range(1, ROWS):
        ar1_copy(j).start()
    ar1[m] = gram[...]
    for j in range(1, ROWS):
        ar1_copy(j).wait()
    total = ar1[0]
    for j in range(1, ROWS):
        total = total + ar1[j]
    gram[...] = total

    place = x * SIDE + z

    def ar2_copy(k):
        dx, dz = others[k]
        return pltpu.make_async_remote_copy(
            src_ref=gram, dst_ref=ar2.at[place], send_sem=ar2_send.at[k], recv_sem=ar2_recv.at[k],
            device_id=plane_peer(dx, dz), device_id_type=MESH)

    for k in range(PLANE - 1):
        ar2_copy(k).start()
    ar2[place] = gram[...]
    for k in range(PLANE - 1):
        ar2_copy(k).wait()
    total = ar2[0]
    for k in range(1, PLANE):
        total = total + ar2[k]

    total_out[...] = jnp.zeros_like(total_out)
    total_out[0:SIDES, :] = total

    for j in range(1, ROWS):
        gather_copy(j).wait_send()
        back_copy(j).wait_send()
    for k in range(1, COLS + 1):
        column_copy(k).wait_send()
        forward_copy(k).wait_send()


def solve_kernel(img24, total_in, solution, residual, direction, new_solution, new_residual, new_direction, dir24, both):
    total = total_in[...]
    img = img24[...]
    dir24[...] = jnp.zeros_like(dir24)
    dir24[0:SIDES, :] = direction[...]
    dirs = dir24[...]
    curv = total[:, 0:SIDES_PAD]
    curv = 0.5 * (curv + curv.T)
    outer = pltpu.roll(total, 96, 1)[:, 0:SIDES_PAD]
    img_res = pltpu.roll(total, 64, 1)[:, 0:SIDES_PAD]
    dir_res = pltpu.roll(total, 32, 1)[:, 0:SIDES_PAD]
    row = lax.broadcasted_iota(jnp.int32, (SIDES_PAD, LANES), 0)
    col = lax.broadcasted_iota(jnp.int32, (SIDES_PAD, LANES), 1)
    both[...] = (col == row + 32).astype(F32)
    both[:, 0:SIDES_PAD] = curv
    work = both[...]
    for i in range(SIDES):
        head = work[i:i + 1, :] * (1.0 / work[i:i + 1, i:i + 1])
        factor = work[:, i:i + 1]
        work = jnp.where(row == i, head, work - factor * head)
    inverse = pltpu.roll(work, 96, 1)[:, 0:SIDES_PAD]

    step_t = exact_dot(dir_res, inverse)
    conj_t = exact_dot(exact_dot(step_t, outer) - img_res, inverse)
    moved = exact_dot(step_t, img)
    new_solution[...] = solution[...] + exact_dot(step_t, dirs)[0:SIDES, :]
    res_new = residual[...] - moved[0:SIDES, :]
    new_residual[...] = res_new
    new_direction[...] = res_new + exact_dot(conj_t, dirs)[0:SIDES, :]


def on_device(points, lengthscale, noise, solution, residual, direction):
    vmem = pl.BlockSpec(memory_space=pltpu.VMEM)
    sem = pltpu.SemaphoreType.DMA
    rows = ROWS * PTS
    image, total = pl.pallas_call(
        kernel,
        out_shape=[jax.ShapeDtypeStruct((SIDES_PAD, PTS), F32), jax.ShapeDtypeStruct((SIDES_PAD, LANES), F32)],
        in_specs=[vmem] * 5,
        out_specs=[vmem] * 2,
        scratch_shapes=[
            pltpu.VMEM((PACKET, PTS), F32),
            pltpu.VMEM((ROWS, PACKET, PTS), F32),
            pltpu.VMEM((COLS + 1, PACKET, PTS), F32),
            pltpu.VMEM((rows, DEPTH), BF16),
            pltpu.VMEM((2 * SIDES_PAD, rows), BF16),
            pltpu.VMEM((SIDES_PAD, rows), F32),
            pltpu.VMEM((LOW, rows), F8),
            pltpu.VMEM((2, SIDES_PAD, LANES), F32),
            pltpu.VMEM((COLS + 1, DEPTH, PTS), BF16),
            pltpu.VMEM((COLS + 1, PTS, LANES), BF16),
            pltpu.VMEM((COLS + 1, PTS, LANES), F8),
            pltpu.VMEM((COLS + 1, 8, LANES), F32),
            pltpu.VMEM((SIDES_PAD, PTS), F32),
            pltpu.VMEM((COLS + 1, 2 * SIDES_PAD, PTS), F32),
            pltpu.VMEM((rows, LANES), F32),
            pltpu.VMEM((COLS + 1, SIDES, PTS), F32),
            pltpu.VMEM((COLS + 1, SIDES, PTS), F32),
            pltpu.VMEM((ROWS, SIDES, PTS), F32),
            pltpu.VMEM((ROWS, SIDES, PTS), F32),
            pltpu.VMEM((SIDES_PAD, PTS), F32),
            pltpu.VMEM((SIDES_PAD, PTS), F32),
            pltpu.VMEM((SIDES, LANES), F32),
            pltpu.VMEM((ROWS, SIDES, LANES), F32),
            pltpu.VMEM((PLANE, SIDES, LANES), F32),
            pltpu.VMEM((SIDES_PAD, PTS), F32),
            sem((ROWS,)), sem((ROWS,)), sem((COLS + 1,)), sem((COLS + 1,)),
            sem((COLS + 1,)), sem((COLS + 1,)), sem((ROWS,)), sem((ROWS,)),
            sem((ROWS,)), sem((ROWS,)), sem((PLANE,)), sem((PLANE,)),
        ],
        compiler_params=pltpu.CompilerParams(
            collective_id=0, has_side_effects=True, vmem_limit_bytes=56 * 2**20
        ),
        cost_estimate=pl.CostEstimate(flops=30_000_000_000, bytes_accessed=1_000_000, transcendentals=34_000_000),
        name="block_cg",
    )(points, lengthscale.reshape(1, FEATS), noise.reshape(1, 1), residual, direction)
    return pl.pallas_call(
        solve_kernel,
        out_shape=[jax.ShapeDtypeStruct((SIDES, PTS), F32)] * 3,
        in_specs=[vmem] * 5,
        out_specs=[vmem] * 3,
        scratch_shapes=[pltpu.VMEM((SIDES_PAD, PTS), F32), pltpu.VMEM((SIDES_PAD, LANES), F32)],
        name="solve",
    )(image, total, solution, residual, direction)


def solution(mesh):
    placed = P(None, ("blk", "narrow"))
    return jax.shard_map(
        on_device,
        mesh=mesh,
        in_specs=(placed, P(), P(), placed, placed, placed),
        out_specs=(placed, placed, placed),
        check_vma=False,
    )
```

```python
import functools
import math

import jax
import jax.numpy as jnp
from jax import lax
from jax.experimental import pallas as pl
from jax.experimental.pallas import tpu as pltpu
from jax.sharding import PartitionSpec as P

BF16 = jnp.bfloat16
F32 = jnp.float32
LN2 = math.log(2.0)
MESH = pl.DeviceIdType.MESH
FEATS = 32
SIDES = 17
SIDES_PAD = 24
PTS = 512
ROWS = 8
PLANE = 16
SIDE = 4
FULL = 6
OFFSETS = ((1, 0), (0, 3), (1, 1), (3, 1), (2, 3), (3, 2), (2, 0), (0, 2), (2, 2))
COLS = len(OFFSETS)
ROW_OFFSETS = ((0, 0), (0, 1), (1, 0), (3, 1), (2, 0), (2, 1), (1, 1), (3, 0))
ROW_Y = tuple(dy for dy, _ in ROW_OFFSETS[1:])
ROW_C = tuple(dc for _, dc in ROW_OFFSETS[1:])
STEP_X = tuple(dx for dx, _ in OFFSETS)
STEP_Z = tuple(dz for _, dz in OFFSETS)
PACKET = 49
DEPTH = 256
CHUNK = 2048
LANES = 128
LOW = 64
BOOST = 14
F8 = jnp.float8_e4m3fn
F8_TOP = 256.0


def dot(left, right, dims=((1,), (0,))):
    return lax.dot_general(left, right, (dims, ((), ())), preferred_element_type=F32)


def exact_dot(left, right, dims=((1,), (0,))):
    return lax.dot_general(
        left, right, (dims, ((), ())), precision=lax.Precision.HIGHEST, preferred_element_type=F32
    )


def split3(x):
    first = x.astype(BF16).astype(F32)
    second = (x - first).astype(BF16).astype(F32)
    third = (x - first - second).astype(BF16).astype(F32)
    return first, second, third


def norm_rows(squares, norms_first):
    s1, s2, s3 = split3(squares)
    row = lax.broadcasted_iota(jnp.int32, (16, PTS), 0)
    zero = jnp.zeros((16, PTS), F32)
    base = 0 if norms_first else 3
    ones = 3 if norms_first else 0
    out = jnp.where((row >= ones) & (row < ones + 3), 1.0, zero)
    for place, part in enumerate((s1, s2, s3)):
        out = jnp.where(row == base + place, jnp.broadcast_to(part, (16, PTS)), out)
    return out


def expand(pts, left):
    p1, p2, p3 = split3(pts)
    squares = jnp.sum(pts * pts, 0, keepdims=True)
    order = (p1, p1, p2, p2, p1, p3) if left else (p1, p2, p1, p2, p3, p1)
    scale = -2.0 if left else 1.0
    rows = [part * scale for part in order]
    rows.append(norm_rows(squares, left))
    rows.append(jnp.zeros((DEPTH - 6 * FEATS - 16, PTS), F32))
    return jnp.concatenate(rows, 0)


def split_dir(rows):
    hi = rows.astype(BF16).astype(F32)
    return jnp.concatenate([hi, rows - hi], 0).astype(BF16)


def matern(q):
    q = jnp.maximum(q, 1e-30)
    t = q * lax.rsqrt(q)
    return ((q + 3.0 / LN2**2) + t * (3.0 / LN2)) * jnp.exp2(BOOST - t)


def pick(k, values):
    if isinstance(k, int):
        return values[k - 1]
    out = values[0]
    for place, value in enumerate(values[1:], 2):
        out = jnp.where(k == place, value, out)
    return out


def kernel(points, lengthscale, noise, residual, direction, img24, total_out,
           pkt, gat, cols, left, ldir, ldirf, ldir8, lscale, right, rdir, rdir8, rscale, side24, fwds, back, rsend, rrecv, bsend, brecv, dir24, res24,
           gram, ar1, ar2, own,
           gat_send, gat_recv, col_send, col_recv, r_send, r_recv, b_send, b_recv,
           ar1_send, ar1_recv, ar2_send, ar2_recv):
    b = lax.axis_index("blk")
    n = lax.axis_index("narrow")

    x = b // 8 * 2 + n % 2
    z = b // 2 % SIDE
    y = n // 2
    c = b % 2
    m = y * 2 + c

    def device(x, z, y, c):
        return (x // 2 * 8 + z * 2 + c, y * 2 + x % 2)

    def row_peer(dy, dc):
        return device(x, z, lax.rem(y + dy, SIDE), lax.rem(c + dc, 2))

    def plane_peer(dx, dz):
        return device(lax.rem(x + dx, SIDE), lax.rem(z + dz, SIDE), y, c)

    others = [(dx, dz) for dx in range(SIDE) for dz in range(SIDE) if dx or dz]

    barrier = pltpu.get_barrier_semaphore()
    for j in range(1, ROWS):
        pl.semaphore_signal(barrier, inc=1, device_id=row_peer(pick(j, ROW_Y), pick(j, ROW_C)), device_id_type=MESH)
    for dx, dz in others:
        pl.semaphore_signal(barrier, inc=1, device_id=plane_peer(dx, dz), device_id_type=MESH)

    dir24[...] = jnp.zeros_like(dir24)
    dir24[0:SIDES, :] = direction[...]
    res24[...] = jnp.zeros_like(res24)
    res24[0:SIDES, :] = residual[...]
    diagonal = lax.broadcasted_iota(jnp.int32, (FEATS, FEATS), 0) == lax.broadcasted_iota(jnp.int32, (FEATS, FEATS), 1)
    lengths = jnp.sum(jnp.where(diagonal, jnp.broadcast_to(lengthscale[...], (FEATS, FEATS)), 0.0), 1, keepdims=True)
    pkt[0:FEATS, :] = points[...] * (math.sqrt(5.0) / LN2 / lengths)
    pkt[FEATS:PACKET, :] = direction[...]
    side24[...] = jnp.zeros_like(side24)
    pl.semaphore_wait(barrier, ROWS + PLANE - 2)

    def gather_copy(j):
        return pltpu.make_async_remote_copy(
            src_ref=pkt, dst_ref=gat.at[j], send_sem=gat_send.at[j], recv_sem=gat_recv.at[j],
            device_id=row_peer(SIDE - pick(j, ROW_Y), pick(j, ROW_C)), device_id_type=MESH)

    def column_copy(k):
        return pltpu.make_async_remote_copy(
            src_ref=pkt, dst_ref=cols.at[k], send_sem=col_send.at[k], recv_sem=col_recv.at[k],
            device_id=plane_peer(SIDE - pick(k, STEP_X), SIDE - pick(k, STEP_Z)), device_id_type=MESH)

    def forward_copy(k):
        return pltpu.make_async_remote_copy(
            src_ref=rsend.at[k], dst_ref=rrecv.at[k], send_sem=r_send.at[k], recv_sem=r_recv.at[k],
            device_id=plane_peer(pick(k, STEP_X), pick(k, STEP_Z)), device_id_type=MESH)

    def back_copy(j):
        return pltpu.make_async_remote_copy(
            src_ref=bsend.at[j], dst_ref=brecv.at[j], send_sem=b_send.at[j], recv_sem=b_recv.at[j],
            device_id=row_peer(pick(j, ROW_Y), pick(j, ROW_C)), device_id_type=MESH)

    middle = ROWS // 2
    for j in range(1, middle):
        gather_copy(j).start()
    for k in range(1, 3):
        column_copy(k).start()

    def padded_sides(packet):
        side24[0:SIDES, :] = packet[FEATS:PACKET, :]
        return side24[...]

    def low_terms(rows, top):
        scaled = rows * (F8_TOP / top)
        first = scaled.astype(F8).astype(F32)
        return first, scaled - first

    def load_right(k, packet):
        right[k] = expand(packet[0:FEATS, :], False).astype(BF16)
        rows = padded_sides(packet)
        hi = rows.astype(BF16).astype(F32)
        top = jnp.maximum(jnp.max(jnp.abs(rows), 1, keepdims=True), 1e-30)
        first, second = low_terms(rows, top)
        scale_rows = jnp.broadcast_to(top * (1.0 / F8_TOP), rows.shape)
        spare = jnp.zeros((LANES - 5 * SIDES_PAD, PTS), F32)
        turned = jnp.concatenate([hi, rows - hi, first, second, scale_rows, spare], 0).T
        lane = lax.broadcasted_iota(jnp.int32, (PTS, LANES), 1)
        rdir[k] = jnp.where(lane < 2 * SIDES_PAD, turned, 0.0).astype(BF16)
        low = (lane >= 2 * SIDES_PAD) & (lane < 4 * SIDES_PAD)
        rdir8[k] = jnp.where(low, turned, 0.0).astype(F8)
        line = turned[0:8, :]
        near = pltpu.roll(line, LANES - SIDES_PAD, 1)
        far = pltpu.roll(line, LANES - 2 * SIDES_PAD, 1)
        rscale[k] = jnp.where(lane[0:8, :] < 3 * SIDES_PAD, far, near)

    def scale_left(half, at):
        rows = ldirf[:, at]
        top = jnp.maximum(jnp.max(jnp.abs(rows), 1, keepdims=True), 1e-30)
        first, second = low_terms(rows, top)
        spare = jnp.zeros((LOW - 2 * SIDES_PAD, rows.shape[1]), F32)
        ldir8[:, at] = jnp.concatenate([first, second, spare], 0).astype(F8)
        lscale[half] = jnp.broadcast_to(top * (1.0 / F8_TOP), (SIDES_PAD, LANES))

    def load_left(j, packet):
        at = pl.ds(pl.multiple_of(j * PTS, PTS), PTS)
        left[at, :] = expand(packet[0:FEATS, :], True).T.astype(BF16)
        rows = padded_sides(packet)
        ldir[:, at] = split_dir(rows)
        ldirf[:, at] = rows

    def tile(k, start, half, both):
        at = pl.ds(pl.multiple_of(start, PTS), CHUNK)
        piece = 512
        waiting = None
        for place in range(0, CHUNK + piece, piece):
            fresh = None
            if place < CHUNK:
                at = pl.ds(pl.multiple_of(start + place, PTS), piece)
                kern = matern(dot(left[at, :], right[k]))
                hi = kern.astype(BF16)
                fresh = at, hi, (kern - hi.astype(F32)).astype(F8)
            if waiting is not None:
                at, hi, lo = waiting
                if both:
                    back[at, :] += dot(hi, rdir[k])
                    back[at, :] += dot(lo, rdir8[k]) * rscale[k, 0:1]
                fwds[k] += dot(ldir[:, at], hi)
                low = dot(ldir8[:, at], lo)
                fwds[k, 0:SIDES_PAD] += (low[0:SIDES_PAD] + low[SIDES_PAD:2 * SIDES_PAD]) * lscale[half, :, 0:1]
            waiting = fresh

    back[...] = jnp.zeros_like(back)
    fwds[...] = jnp.zeros_like(fwds)
    right[0] = expand(pkt[0:FEATS, :], False).astype(BF16)
    load_left(0, pkt)

    @pl.loop(1, middle)
    def _(j):
        gather_copy(j).wait_recv()
        load_left(j, gat.at[j])

    for k in range(3, COLS + 1):
        column_copy(k).start()
    scale_left(0, pl.ds(0, middle * PTS))
    upper_x = jnp.where(x >= SIDE // 2, 2 * PTS, 0)
    upper_z = jnp.where(z >= SIDE // 2, 2 * PTS, 0)

    def back_slice(j):
        part = back[pl.ds(pl.multiple_of(j * PTS, PTS), PTS), :].T
        return sum(part[i * SIDES_PAD:i * SIDES_PAD + SIDES, :] for i in range(4))

    def send_back(first, last):
        @pl.loop(first, last)
        def _(j):
            bsend[j] = back_slice(j)
            back_copy(j).start()

    @pl.loop(0, COLS + FULL)
    def _(s):
        first = s < COLS
        k = jnp.where(first, s + 1, COLS + FULL - s)

        @pl.when(first)
        def _():
            column_copy(k).wait_recv()
            load_right(k, cols.at[k])

        @pl.when(s < ROWS - middle)
        def _():
            gather_copy(s + middle).start()

        @pl.when(s == FULL)
        def _():
            @pl.loop(middle, middle + 2)
            def _(j):
                gather_copy(j).wait_recv()
                load_left(j, gat.at[j])

            scale_left(0, pl.ds(0, (middle + 2) * PTS))

        @pl.when(s == COLS)
        def _():
            @pl.loop(middle + 2, ROWS)
            def _(j):
                gather_copy(j).wait_recv()
                load_left(j, gat.at[j])

            scale_left(1, pl.ds(middle * PTS, (ROWS - middle) * PTS))
            send_back(1, middle)

        upper = jnp.where(k == FULL + 2, upper_z, upper_x)
        tile(k, jnp.where(first, jnp.where(k > FULL, upper, 0), CHUNK), jnp.where(first, 0, 1), True)

        @pl.when(s >= FULL)
        def _():
            rsend[k] = fwds[k, 0:SIDES] + fwds[k, SIDES_PAD:SIDES_PAD + SIDES]
            forward_copy(k).start()

    send_back(middle, ROWS)

    @pl.loop(0, 2)
    def _(half):
        tile(0, half * CHUNK, half, False)

    own[...] = fwds[0, 0:SIDES_PAD] + fwds[0, SIDES_PAD:]
    own[0:SIDES, :] += back_slice(0)
    for k in range(1, COLS + 1):
        forward_copy(k).wait_recv()
        own[0:SIDES, :] += rrecv[k]
    for j in range(1, ROWS):
        back_copy(j).wait_recv()
        own[0:SIDES, :] += brecv[j]
    img24[...] = own[...] * (LN2 * LN2 / 3.0 / 2.0**BOOST) + noise[...] * dir24[...]

    zeros8 = jnp.zeros((8, PTS), F32)
    zeros64 = jnp.zeros((64, PTS), F32)
    img, dirs, res = img24[...], dir24[...], res24[...]
    table = jnp.concatenate([dirs, zeros8, img, zeros8, zeros64], 0)
    other = jnp.concatenate([zeros64, img, zeros8, dirs, zeros8], 0)
    gram[...] = (exact_dot(img, table, ((1,), (1,))) + exact_dot(res, other, ((1,), (1,))))[0:SIDES, :]

    def ar1_copy(j):
        return pltpu.make_async_remote_copy(
            src_ref=gram, dst_ref=ar1.at[m], send_sem=ar1_send.at[j], recv_sem=ar1_recv.at[j],
            device_id=row_peer(pick(j, ROW_Y), pick(j, ROW_C)), device_id_type=MESH)

    for j in range(1, ROWS):
        ar1_copy(j).start()
    ar1[m] = gram[...]
    for j in range(1, ROWS):
        ar1_copy(j).wait()
    total = ar1[0]
    for j in range(1, ROWS):
        total = total + ar1[j]
    gram[...] = total

    place = x * SIDE + z

    def ar2_copy(k):
        dx, dz = others[k]
        return pltpu.make_async_remote_copy(
            src_ref=gram, dst_ref=ar2.at[place], send_sem=ar2_send.at[k], recv_sem=ar2_recv.at[k],
            device_id=plane_peer(dx, dz), device_id_type=MESH)

    for k in range(PLANE - 1):
        ar2_copy(k).start()
    ar2[place] = gram[...]
    for k in range(PLANE - 1):
        ar2_copy(k).wait()
    total = ar2[0]
    for k in range(1, PLANE):
        total = total + ar2[k]

    total_out[...] = jnp.zeros_like(total_out)
    total_out[0:SIDES, :] = total

    for j in range(1, ROWS):
        gather_copy(j).wait_send()
        back_copy(j).wait_send()
    for k in range(1, COLS + 1):
        column_copy(k).wait_send()
        forward_copy(k).wait_send()


def solve_kernel(img24, total_in, solution, residual, direction, new_solution, new_residual, new_direction, dir24, both):
    total = total_in[...]
    img = img24[...]
    dir24[...] = jnp.zeros_like(dir24)
    dir24[0:SIDES, :] = direction[...]
    dirs = dir24[...]
    curv = total[:, 0:SIDES_PAD]
    curv = 0.5 * (curv + curv.T)
    outer = pltpu.roll(total, 96, 1)[:, 0:SIDES_PAD]
    img_res = pltpu.roll(total, 64, 1)[:, 0:SIDES_PAD]
    dir_res = pltpu.roll(total, 32, 1)[:, 0:SIDES_PAD]
    row = lax.broadcasted_iota(jnp.int32, (SIDES_PAD, LANES), 0)
    col = lax.broadcasted_iota(jnp.int32, (SIDES_PAD, LANES), 1)
    both[...] = (col == row + 32).astype(F32)
    both[:, 0:SIDES_PAD] = curv
    work = both[...]
    for i in range(SIDES):
        head = work[i:i + 1, :] * (1.0 / work[i:i + 1, i:i + 1])
        factor = work[:, i:i + 1]
        work = jnp.where(row == i, head, work - factor * head)
    inverse = pltpu.roll(work, 96, 1)[:, 0:SIDES_PAD]

    step_t = exact_dot(dir_res, inverse)
    reach = exact_dot(inverse, dirs)
    conj_left = exact_dot(step_t, outer) - img_res
    moved = exact_dot(step_t, img)
    new_solution[...] = solution[...] + exact_dot(dir_res, reach)[0:SIDES, :]
    res_new = residual[...] - moved[0:SIDES, :]
    new_residual[...] = res_new
    new_direction[...] = res_new + exact_dot(conj_left, reach)[0:SIDES, :]


def on_device(points, lengthscale, noise, solution, residual, direction):
    vmem = pl.BlockSpec(memory_space=pltpu.VMEM)
    sem = pltpu.SemaphoreType.DMA
    rows = ROWS * PTS
    image, total = pl.pallas_call(
        kernel,
        out_shape=[jax.ShapeDtypeStruct((SIDES_PAD, PTS), F32), jax.ShapeDtypeStruct((SIDES_PAD, LANES), F32)],
        in_specs=[vmem] * 5,
        out_specs=[vmem] * 2,
        scratch_shapes=[
            pltpu.VMEM((PACKET, PTS), F32),
            pltpu.VMEM((ROWS, PACKET, PTS), F32),
            pltpu.VMEM((COLS + 1, PACKET, PTS), F32),
            pltpu.VMEM((rows, DEPTH), BF16),
            pltpu.VMEM((2 * SIDES_PAD, rows), BF16),
            pltpu.VMEM((SIDES_PAD, rows), F32),
            pltpu.VMEM((LOW, rows), F8),
            pltpu.VMEM((2, SIDES_PAD, LANES), F32),
            pltpu.VMEM((COLS + 1, DEPTH, PTS), BF16),
            pltpu.VMEM((COLS + 1, PTS, LANES), BF16),
            pltpu.VMEM((COLS + 1, PTS, LANES), F8),
            pltpu.VMEM((COLS + 1, 8, LANES), F32),
            pltpu.VMEM((SIDES_PAD, PTS), F32),
            pltpu.VMEM((COLS + 1, 2 * SIDES_PAD, PTS), F32),
            pltpu.VMEM((rows, LANES), F32),
            pltpu.VMEM((COLS + 1, SIDES, PTS), F32),
            pltpu.VMEM((COLS + 1, SIDES, PTS), F32),
            pltpu.VMEM((ROWS, SIDES, PTS), F32),
            pltpu.VMEM((ROWS, SIDES, PTS), F32),
            pltpu.VMEM((SIDES_PAD, PTS), F32),
            pltpu.VMEM((SIDES_PAD, PTS), F32),
            pltpu.VMEM((SIDES, LANES), F32),
            pltpu.VMEM((ROWS, SIDES, LANES), F32),
            pltpu.VMEM((PLANE, SIDES, LANES), F32),
            pltpu.VMEM((SIDES_PAD, PTS), F32),
            sem((ROWS,)), sem((ROWS,)), sem((COLS + 1,)), sem((COLS + 1,)),
            sem((COLS + 1,)), sem((COLS + 1,)), sem((ROWS,)), sem((ROWS,)),
            sem((ROWS,)), sem((ROWS,)), sem((PLANE,)), sem((PLANE,)),
        ],
        compiler_params=pltpu.CompilerParams(
            collective_id=0, has_side_effects=True, vmem_limit_bytes=56 * 2**20
        ),
        cost_estimate=pl.CostEstimate(flops=30_000_000_000, bytes_accessed=1_000_000, transcendentals=34_000_000),
        name="block_cg",
    )(points, lengthscale.reshape(1, FEATS), noise.reshape(1, 1), residual, direction)
    return pl.pallas_call(
        solve_kernel,
        out_shape=[jax.ShapeDtypeStruct((SIDES, PTS), F32)] * 3,
        in_specs=[vmem] * 5,
        out_specs=[vmem] * 3,
        scratch_shapes=[pltpu.VMEM((SIDES_PAD, PTS), F32), pltpu.VMEM((SIDES_PAD, LANES), F32)],
        name="solve",
    )(image, total, solution, residual, direction)


def solution(mesh):
    placed = P(None, ("blk", "narrow"))
    return jax.shard_map(
        on_device,
        mesh=mesh,
        in_specs=(placed, P(), P(), placed, placed, placed),
        out_specs=(placed, placed, placed),
        check_vma=False,
    )
```

```python
import functools
import math

import jax
import jax.numpy as jnp
from jax import lax
from jax.experimental import pallas as pl
from jax.experimental.pallas import tpu as pltpu
from jax.sharding import PartitionSpec as P

BF16 = jnp.bfloat16
F32 = jnp.float32
LN2 = math.log(2.0)
MESH = pl.DeviceIdType.MESH
FEATS = 32
SIDES = 17
SIDES_PAD = 24
PTS = 512
ROWS = 8
PLANE = 16
SIDE = 4
FULL = 6
OFFSETS = ((1, 0), (0, 3), (1, 1), (3, 1), (2, 3), (3, 2), (2, 0), (0, 2), (2, 2))
COLS = len(OFFSETS)
ROW_OFFSETS = ((0, 0), (0, 1), (1, 0), (3, 1), (2, 0), (2, 1), (1, 1), (3, 0))
ROW_Y = tuple(dy for dy, _ in ROW_OFFSETS[1:])
ROW_C = tuple(dc for _, dc in ROW_OFFSETS[1:])
STEP_X = tuple(dx for dx, _ in OFFSETS)
STEP_Z = tuple(dz for _, dz in OFFSETS)
PACKET = 49
DEPTH = 256
CHUNK = 2048
LANES = 128
LOW = 64
BOOST = 14
F8 = jnp.float8_e4m3fn
F8_TOP = 256.0


def dot(left, right, dims=((1,), (0,))):
    return lax.dot_general(left, right, (dims, ((), ())), preferred_element_type=F32)


def exact_dot(left, right, dims=((1,), (0,))):
    return lax.dot_general(
        left, right, (dims, ((), ())), precision=lax.Precision.HIGHEST, preferred_element_type=F32
    )


def split3(x):
    first = x.astype(BF16).astype(F32)
    second = (x - first).astype(BF16).astype(F32)
    third = (x - first - second).astype(BF16).astype(F32)
    return first, second, third


def norm_rows(squares, norms_first):
    s1, s2, s3 = split3(squares)
    row = lax.broadcasted_iota(jnp.int32, (16, PTS), 0)
    zero = jnp.zeros((16, PTS), F32)
    base = 0 if norms_first else 3
    ones = 3 if norms_first else 0
    out = jnp.where((row >= ones) & (row < ones + 3), 1.0, zero)
    for place, part in enumerate((s1, s2, s3)):
        out = jnp.where(row == base + place, jnp.broadcast_to(part, (16, PTS)), out)
    return out


def expand(pts, left):
    p1, p2, p3 = split3(pts)
    squares = jnp.sum(pts * pts, 0, keepdims=True)
    order = (p1, p1, p2, p2, p1, p3) if left else (p1, p2, p1, p2, p3, p1)
    scale = -2.0 if left else 1.0
    rows = [part * scale for part in order]
    rows.append(norm_rows(squares, left))
    rows.append(jnp.zeros((DEPTH - 6 * FEATS - 16, PTS), F32))
    return jnp.concatenate(rows, 0)


def split_dir(rows):
    hi = rows.astype(BF16).astype(F32)
    return jnp.concatenate([hi, rows - hi], 0).astype(BF16)


def matern(q):
    q = jnp.maximum(q, 1e-30)
    t = q * lax.rsqrt(q)
    return ((q + 3.0 / LN2**2) + t * (3.0 / LN2)) * jnp.exp2(BOOST - t)


def pick(k, values):
    if isinstance(k, int):
        return values[k - 1]
    out = values[0]
    for place, value in enumerate(values[1:], 2):
        out = jnp.where(k == place, value, out)
    return out


def kernel(points, lengthscale, noise, residual, direction, img24, total_out,
           pkt, gat, cols, left, ldir, ldirf, ldir8, lscale, right, rdir, rdir8, rscale, side24, fwds, back, rsend, rrecv, bsend, brecv, dir24, res24,
           gram, ar1, ar2, own, early,
           gat_send, gat_recv, col_send, col_recv, r_send, r_recv, b_send, b_recv,
           ar1_send, ar1_recv, ar2_send, ar2_recv):
    b = lax.axis_index("blk")
    n = lax.axis_index("narrow")

    x = b // 8 * 2 + n % 2
    z = b // 2 % SIDE
    y = n // 2
    c = b % 2
    m = y * 2 + c

    def device(x, z, y, c):
        return (x // 2 * 8 + z * 2 + c, y * 2 + x % 2)

    def row_peer(dy, dc):
        return device(x, z, lax.rem(y + dy, SIDE), lax.rem(c + dc, 2))

    def plane_peer(dx, dz):
        return device(lax.rem(x + dx, SIDE), lax.rem(z + dz, SIDE), y, c)

    others = [(dx, dz) for dx in range(SIDE) for dz in range(SIDE) if dx or dz]

    barrier = pltpu.get_barrier_semaphore()
    for j in range(1, ROWS):
        pl.semaphore_signal(barrier, inc=1, device_id=row_peer(pick(j, ROW_Y), pick(j, ROW_C)), device_id_type=MESH)
    for dx, dz in others:
        pl.semaphore_signal(barrier, inc=1, device_id=plane_peer(dx, dz), device_id_type=MESH)

    dir24[...] = jnp.zeros_like(dir24)
    dir24[0:SIDES, :] = direction[...]
    res24[...] = jnp.zeros_like(res24)
    res24[0:SIDES, :] = residual[...]
    diagonal = lax.broadcasted_iota(jnp.int32, (FEATS, FEATS), 0) == lax.broadcasted_iota(jnp.int32, (FEATS, FEATS), 1)
    lengths = jnp.sum(jnp.where(diagonal, jnp.broadcast_to(lengthscale[...], (FEATS, FEATS)), 0.0), 1, keepdims=True)
    pkt[0:FEATS, :] = points[...] * (math.sqrt(5.0) / LN2 / lengths)
    pkt[FEATS:PACKET, :] = direction[...]
    side24[...] = jnp.zeros_like(side24)
    pl.semaphore_wait(barrier, ROWS + PLANE - 2)

    def gather_copy(j):
        return pltpu.make_async_remote_copy(
            src_ref=pkt, dst_ref=gat.at[j], send_sem=gat_send.at[j], recv_sem=gat_recv.at[j],
            device_id=row_peer(SIDE - pick(j, ROW_Y), pick(j, ROW_C)), device_id_type=MESH)

    def column_copy(k):
        return pltpu.make_async_remote_copy(
            src_ref=pkt, dst_ref=cols.at[k], send_sem=col_send.at[k], recv_sem=col_recv.at[k],
            device_id=plane_peer(SIDE - pick(k, STEP_X), SIDE - pick(k, STEP_Z)), device_id_type=MESH)

    def forward_copy(k):
        return pltpu.make_async_remote_copy(
            src_ref=rsend.at[k], dst_ref=rrecv.at[k], send_sem=r_send.at[k], recv_sem=r_recv.at[k],
            device_id=plane_peer(pick(k, STEP_X), pick(k, STEP_Z)), device_id_type=MESH)

    def back_copy(j):
        return pltpu.make_async_remote_copy(
            src_ref=bsend.at[j], dst_ref=brecv.at[j], send_sem=b_send.at[j], recv_sem=b_recv.at[j],
            device_id=row_peer(pick(j, ROW_Y), pick(j, ROW_C)), device_id_type=MESH)

    middle = ROWS // 2
    for j in range(1, middle):
        gather_copy(j).start()
    for k in range(1, 3):
        column_copy(k).start()

    def padded_sides(packet):
        side24[0:SIDES, :] = packet[FEATS:PACKET, :]
        return side24[...]

    def low_terms(rows, top):
        scaled = rows * (F8_TOP / top)
        first = scaled.astype(F8).astype(F32)
        return first, scaled - first

    def load_right(k, packet):
        right[k] = expand(packet[0:FEATS, :], False).astype(BF16)
        rows = padded_sides(packet)
        hi = rows.astype(BF16).astype(F32)
        top = jnp.maximum(jnp.max(jnp.abs(rows), 1, keepdims=True), 1e-30)
        first, second = low_terms(rows, top)
        scale_rows = jnp.broadcast_to(top * (1.0 / F8_TOP), rows.shape)
        spare = jnp.zeros((LANES - 5 * SIDES_PAD, PTS), F32)
        turned = jnp.concatenate([hi, rows - hi, first, second, scale_rows, spare], 0).T
        lane = lax.broadcasted_iota(jnp.int32, (PTS, LANES), 1)
        rdir[k] = jnp.where(lane < 2 * SIDES_PAD, turned, 0.0).astype(BF16)
        low = (lane >= 2 * SIDES_PAD) & (lane < 4 * SIDES_PAD)
        rdir8[k] = jnp.where(low, turned, 0.0).astype(F8)
        line = turned[0:8, :]
        near = pltpu.roll(line, LANES - SIDES_PAD, 1)
        far = pltpu.roll(line, LANES - 2 * SIDES_PAD, 1)
        rscale[k] = jnp.where(lane[0:8, :] < 3 * SIDES_PAD, far, near)

    def scale_left(half, at):
        rows = ldirf[:, at]
        top = jnp.maximum(jnp.max(jnp.abs(rows), 1, keepdims=True), 1e-30)
        first, second = low_terms(rows, top)
        spare = jnp.zeros((LOW - 2 * SIDES_PAD, rows.shape[1]), F32)
        ldir8[:, at] = jnp.concatenate([first, second, spare], 0).astype(F8)
        lscale[half] = jnp.broadcast_to(top * (1.0 / F8_TOP), (SIDES_PAD, LANES))

    def load_left(j, packet):
        at = pl.ds(pl.multiple_of(j * PTS, PTS), PTS)
        left[at, :] = expand(packet[0:FEATS, :], True).T.astype(BF16)
        rows = padded_sides(packet)
        ldir[:, at] = split_dir(rows)
        ldirf[:, at] = rows

    def tile(k, start, half, both):
        at = pl.ds(pl.multiple_of(start, PTS), CHUNK)
        piece = 512
        waiting = None
        for place in range(0, CHUNK + piece, piece):
            fresh = None
            if place < CHUNK:
                at = pl.ds(pl.multiple_of(start + place, PTS), piece)
                kern = matern(dot(left[at, :], right[k]))
                hi = kern.astype(BF16)
                fresh = at, hi, (kern - hi.astype(F32)).astype(F8)
            if waiting is not None:
                at, hi, lo = waiting
                if both:
                    back[at, :] += dot(hi, rdir[k])
                    back[at, :] += dot(lo, rdir8[k]) * rscale[k, 0:1]
                fwds[k] += dot(ldir[:, at], hi)
                low = dot(ldir8[:, at], lo)
                fwds[k, 0:SIDES_PAD] += (low[0:SIDES_PAD] + low[SIDES_PAD:2 * SIDES_PAD]) * lscale[half, :, 0:1]
            waiting = fresh

    other = jnp.concatenate([jnp.zeros((96, PTS), F32), dir24[...], jnp.zeros((8, PTS), F32)], 0)
    early[...] = exact_dot(res24[...], other, ((1,), (1,)))
    back[...] = jnp.zeros_like(back)
    fwds[...] = jnp.zeros_like(fwds)
    right[0] = expand(pkt[0:FEATS, :], False).astype(BF16)
    load_left(0, pkt)

    @pl.loop(1, middle)
    def _(j):
        gather_copy(j).wait_recv()
        load_left(j, gat.at[j])

    for k in range(3, COLS + 1):
        column_copy(k).start()
    scale_left(0, pl.ds(0, middle * PTS))
    upper_x = jnp.where(x >= SIDE // 2, 2 * PTS, 0)
    upper_z = jnp.where(z >= SIDE // 2, 2 * PTS, 0)

    def back_slice(j):
        part = back[pl.ds(pl.multiple_of(j * PTS, PTS), PTS), :].T
        return sum(part[i * SIDES_PAD:i * SIDES_PAD + SIDES, :] for i in range(4))

    def send_back(first, last):
        @pl.loop(first, last)
        def _(j):
            bsend[j] = back_slice(j)
            back_copy(j).start()

    @pl.loop(0, COLS + FULL)
    def _(s):
        first = s < COLS
        k = jnp.where(first, s + 1, COLS + FULL - s)

        @pl.when(first)
        def _():
            column_copy(k).wait_recv()
            load_right(k, cols.at[k])

        @pl.when(s < ROWS - middle)
        def _():
            gather_copy(s + middle).start()

        @pl.when(s == FULL)
        def _():
            @pl.loop(middle, middle + 2)
            def _(j):
                gather_copy(j).wait_recv()
                load_left(j, gat.at[j])

            scale_left(0, pl.ds(0, (middle + 2) * PTS))

        @pl.when(s == COLS)
        def _():
            @pl.loop(middle + 2, ROWS)
            def _(j):
                gather_copy(j).wait_recv()
                load_left(j, gat.at[j])

            scale_left(1, pl.ds(middle * PTS, (ROWS - middle) * PTS))
            send_back(1, middle)

        upper = jnp.where(k == FULL + 2, upper_z, upper_x)
        tile(k, jnp.where(first, jnp.where(k > FULL, upper, 0), CHUNK), jnp.where(first, 0, 1), True)

        @pl.when(s >= FULL)
        def _():
            rsend[k] = fwds[k, 0:SIDES] + fwds[k, SIDES_PAD:SIDES_PAD + SIDES]
            forward_copy(k).start()

    send_back(middle, ROWS)

    @pl.loop(0, 2)
    def _(half):
        tile(0, half * CHUNK, half, False)

    own[...] = fwds[0, 0:SIDES_PAD] + fwds[0, SIDES_PAD:]
    own[0:SIDES, :] += back_slice(0)
    for k in range(1, COLS + 1):
        forward_copy(k).wait_recv()
        own[0:SIDES, :] += rrecv[k]
    for j in range(1, ROWS):
        back_copy(j).wait_recv()
        own[0:SIDES, :] += brecv[j]
    img24[...] = own[...] * (LN2 * LN2 / 3.0 / 2.0**BOOST) + noise[...] * dir24[...]

    img = img24[...]
    table = jnp.concatenate([img, jnp.zeros((LANES - SIDES_PAD, PTS), F32)], 0)
    products = exact_dot(jnp.concatenate([dir24[...], img, res24[...]], 0), table, ((1,), (1,)))
    near = pltpu.roll(products[SIDES_PAD:2 * SIDES_PAD], 32, 1)
    far = pltpu.roll(products[2 * SIDES_PAD:3 * SIDES_PAD], 64, 1)
    gram[...] = (products[0:SIDES_PAD] + near + far + early[...])[0:SIDES, :]

    def ar1_copy(j):
        return pltpu.make_async_remote_copy(
            src_ref=gram, dst_ref=ar1.at[m], send_sem=ar1_send.at[j], recv_sem=ar1_recv.at[j],
            device_id=row_peer(pick(j, ROW_Y), pick(j, ROW_C)), device_id_type=MESH)

    for j in range(1, ROWS):
        ar1_copy(j).start()
    ar1[m] = gram[...]
    for j in range(1, ROWS):
        ar1_copy(j).wait()
    total = ar1[0]
    for j in range(1, ROWS):
        total = total + ar1[j]
    gram[...] = total

    place = x * SIDE + z

    def ar2_copy(k):
        dx, dz = others[k]
        return pltpu.make_async_remote_copy(
            src_ref=gram, dst_ref=ar2.at[place], send_sem=ar2_send.at[k], recv_sem=ar2_recv.at[k],
            device_id=plane_peer(dx, dz), device_id_type=MESH)

    for k in range(PLANE - 1):
        ar2_copy(k).start()
    ar2[place] = gram[...]
    for k in range(PLANE - 1):
        ar2_copy(k).wait()
    total = ar2[0]
    for k in range(1, PLANE):
        total = total + ar2[k]

    total_out[...] = jnp.zeros_like(total_out)
    total_out[0:SIDES, :] = total

    for j in range(1, ROWS):
        gather_copy(j).wait_send()
        back_copy(j).wait_send()
    for k in range(1, COLS + 1):
        column_copy(k).wait_send()
        forward_copy(k).wait_send()


def solve_kernel(img24, total_in, solution, residual, direction, new_solution, new_residual, new_direction, dir24, both):
    total = total_in[...]
    img = img24[...]
    dir24[...] = jnp.zeros_like(dir24)
    dir24[0:SIDES, :] = direction[...]
    dirs = dir24[...]
    curv = total[:, 0:SIDES_PAD]
    curv = 0.5 * (curv + curv.T)
    outer = pltpu.roll(total, 96, 1)[:, 0:SIDES_PAD]
    img_res = pltpu.roll(total, 64, 1)[:, 0:SIDES_PAD]
    dir_res = pltpu.roll(total, 32, 1)[:, 0:SIDES_PAD]
    row = lax.broadcasted_iota(jnp.int32, (SIDES_PAD, LANES), 0)
    col = lax.broadcasted_iota(jnp.int32, (SIDES_PAD, LANES), 1)
    both[...] = (col == row + 32).astype(F32)
    both[:, 0:SIDES_PAD] = curv
    work = both[...]
    for i in range(SIDES):
        head = work[i:i + 1, :] * (1.0 / work[i:i + 1, i:i + 1])
        factor = work[:, i:i + 1]
        work = jnp.where(row == i, head, work - factor * head)
    inverse = pltpu.roll(work, 96, 1)[:, 0:SIDES_PAD]

    step_t = exact_dot(dir_res, inverse)
    reach = exact_dot(inverse, dirs)
    conj_left = exact_dot(step_t, outer) - img_res
    moved = exact_dot(step_t, img)
    new_solution[...] = solution[...] + exact_dot(dir_res, reach)[0:SIDES, :]
    res_new = residual[...] - moved[0:SIDES, :]
    new_residual[...] = res_new
    new_direction[...] = res_new + exact_dot(conj_left, reach)[0:SIDES, :]


def on_device(points, lengthscale, noise, solution, residual, direction):
    vmem = pl.BlockSpec(memory_space=pltpu.VMEM)
    sem = pltpu.SemaphoreType.DMA
    rows = ROWS * PTS
    image, total = pl.pallas_call(
        kernel,
        out_shape=[jax.ShapeDtypeStruct((SIDES_PAD, PTS), F32), jax.ShapeDtypeStruct((SIDES_PAD, LANES), F32)],
        in_specs=[vmem] * 5,
        out_specs=[vmem] * 2,
        scratch_shapes=[
            pltpu.VMEM((PACKET, PTS), F32),
            pltpu.VMEM((ROWS, PACKET, PTS), F32),
            pltpu.VMEM((COLS + 1, PACKET, PTS), F32),
            pltpu.VMEM((rows, DEPTH), BF16),
            pltpu.VMEM((2 * SIDES_PAD, rows), BF16),
            pltpu.VMEM((SIDES_PAD, rows), F32),
            pltpu.VMEM((LOW, rows), F8),
            pltpu.VMEM((2, SIDES_PAD, LANES), F32),
            pltpu.VMEM((COLS + 1, DEPTH, PTS), BF16),
            pltpu.VMEM((COLS + 1, PTS, LANES), BF16),
            pltpu.VMEM((COLS + 1, PTS, LANES), F8),
            pltpu.VMEM((COLS + 1, 8, LANES), F32),
            pltpu.VMEM((SIDES_PAD, PTS), F32),
            pltpu.VMEM((COLS + 1, 2 * SIDES_PAD, PTS), F32),
            pltpu.VMEM((rows, LANES), F32),
            pltpu.VMEM((COLS + 1, SIDES, PTS), F32),
            pltpu.VMEM((COLS + 1, SIDES, PTS), F32),
            pltpu.VMEM((ROWS, SIDES, PTS), F32),
            pltpu.VMEM((ROWS, SIDES, PTS), F32),
            pltpu.VMEM((SIDES_PAD, PTS), F32),
            pltpu.VMEM((SIDES_PAD, PTS), F32),
            pltpu.VMEM((SIDES, LANES), F32),
            pltpu.VMEM((ROWS, SIDES, LANES), F32),
            pltpu.VMEM((PLANE, SIDES, LANES), F32),
            pltpu.VMEM((SIDES_PAD, PTS), F32),
            pltpu.VMEM((SIDES_PAD, LANES), F32),
            sem((ROWS,)), sem((ROWS,)), sem((COLS + 1,)), sem((COLS + 1,)),
            sem((COLS + 1,)), sem((COLS + 1,)), sem((ROWS,)), sem((ROWS,)),
            sem((ROWS,)), sem((ROWS,)), sem((PLANE,)), sem((PLANE,)),
        ],
        compiler_params=pltpu.CompilerParams(
            collective_id=0, has_side_effects=True, vmem_limit_bytes=56 * 2**20
        ),
        cost_estimate=pl.CostEstimate(flops=30_000_000_000, bytes_accessed=1_000_000, transcendentals=34_000_000),
        name="block_cg",
    )(points, lengthscale.reshape(1, FEATS), noise.reshape(1, 1), residual, direction)
    return pl.pallas_call(
        solve_kernel,
        out_shape=[jax.ShapeDtypeStruct((SIDES, PTS), F32)] * 3,
        in_specs=[vmem] * 5,
        out_specs=[vmem] * 3,
        scratch_shapes=[pltpu.VMEM((SIDES_PAD, PTS), F32), pltpu.VMEM((SIDES_PAD, LANES), F32)],
        name="solve",
    )(image, total, solution, residual, direction)


def solution(mesh):
    placed = P(None, ("blk", "narrow"))
    return jax.shard_map(
        on_device,
        mesh=mesh,
        in_specs=(placed, P(), P(), placed, placed, placed),
        out_specs=(placed, placed, placed),
        check_vma=False,
    )
```
